512 devices in a mesh: geo: 64 (over z, y), cell: 8 (over x, core).
Axes of the slice: x: 4, y: 4, z: 16, core: 2. Of those that a mesh axis runs over, the one named last changes fastest.
Arguments:
- detail_rows: float32 [8192, 2048], P('geo', 'cell'), may hold values from -60 to 60
- row_block: int32 [8192], P('geo'), may hold values from 0 to 8191, as said below
- block_weight: int32 [8192], P('geo'), may hold values from 1 to 9
- block_group: int32 [8192], P('geo'), may hold values from 0 to 63, as said below
- query_matrix: int32 [2048, 512], P('cell'), may hold values 0 or 1
- query_weight: float32 [512], replicated, may hold values from 0.0048828125 to 0.048828125
- query_noisy: float32 [8192, 512], P('geo'), may hold values from -48 to 48
- group_noisy: float32 [64, 2048], P(None, 'cell'), may hold values from -48 to 48
Outputs:
- solution_field: float32 [8192, 2048], P('geo', 'cell')
- residual: float32 [8192, 2048], P('geo', 'cell')
The draws below stay inside these ranges and needn't reach their ends.
Inputs may be any that keep to these rules, and one draw needn't show every extreme that they name: row_block is a permutation of all blocks; arrival row r lies on geo index r // 128 and its block lies on geo index (r mod 128) // 2, so each geo index sends 2 rows to each geo index. `block_group`: every group holds exactly 128 blocks.
All inputs are finite; a program needn't handle non-finite values. No bound on the sum of `query_matrix` on one device may be relied on, other than what follows from the above.
Results may differ from the reference program's by a relative error of at most 0.0029.
Values sent between devices are 32-bit elements; how exact they have to be, the bound alone decides.
A program may use at most 64 MiB of HBM per device.

```python
import math
import jax
import jax.numpy as jnp
from jax import lax

CELLS = 2048
QUERIES = 512
GROUP_SIZE = 128
ITERS = 2
BLK_DEV = 128
BLOCKS = 8192
GROUPS = 64
SEND = 2


def arrival_blocks(key):
    base_key = jax.random.fold_in(key, 17)
    geo_count = BLOCKS // BLK_DEV
    dest_keys = jax.random.split(base_key, geo_count)
    orders = jax.vmap(lambda one_key: jax.random.permutation(one_key, BLK_DEV))(dest_keys)
    block_ids = orders + (jnp.arange(geo_count) * BLK_DEV)[:, None]
    block_ids = block_ids.reshape(geo_count, geo_count, SEND)
    return jnp.transpose(block_ids, (1, 0, 2)).reshape(BLOCKS).astype(jnp.int32)


def draw_row_block(key, part):
    return arrival_blocks(key)


def draw_block_group(key, part):
    shuffled = jax.random.permutation(jax.random.fold_in(key, 41), BLOCKS)
    return (shuffled // GROUP_SIZE).astype(jnp.int32)


def draw_detail_rows(key, part):
    block_ids = arrival_blocks(key)
    noise_key, row_key, col_key = jax.random.split(jax.random.fold_in(key, 29), 3)
    position = block_ids.astype(jnp.float32) / BLOCKS
    row_scale = jnp.exp(jnp.log(3.0) * position) * jnp.exp(jnp.log(4.0) * jax.random.uniform(row_key, (BLOCKS,)))
    col_scale = jnp.exp(jnp.log(10.0) * jax.random.uniform(col_key, (CELLS,)))
    noise_core = jnp.clip(jax.random.normal(noise_key, (BLOCKS, CELLS)), -5.0, 5.0)
    return (noise_core * row_scale[:, None] * col_scale[None, :] / 10.0).astype(jnp.float32)


def with_ends(array, stream_key, smallest, top_value):
    extent = array.shape
    index_at = [jax.random.randint(jax.random.fold_in(stream_key, axis), (), 0, extent[axis]) for axis in range(len(extent))]
    array = array.at[tuple(index_at)].set(smallest)
    longest = extent.index(max(extent))
    index_at[longest] = (index_at[longest] + 1) % extent[longest]
    return array.at[tuple(index_at)].set(top_value)


def levels(key, shape, shards, least, high):
    def one(axis_at, shards_of):
        draws = jax.random.uniform(jax.random.fold_in(jax.random.fold_in(key, 6), axis_at), (shards_of,), jnp.float32, least / len(shards), high / len(shards))
        return jnp.repeat(jnp.exp(draws), shape[axis_at] // shards_of).reshape((-1,) + (1,) * (len(shape) - axis_at - 1))

    gain = one(*shards[0])
    for cut in shards[1:]:
        gain = gain * one(*cut)
    return gain


def centred(stream_key, extent, deviation, bound, cuts=(), kind=jnp.bfloat16):
    result = jax.random.normal(stream_key, extent, jnp.float32) * deviation
    if len(cuts) > 0:
        result = levels(stream_key, extent, cuts, -0.22, 0.18) * result
    return jnp.clip(result, min=-bound, max=bound).astype(kind)


def setup_inputs(seed: int = 0) -> dict:
    streams_of = jax.random.split(jax.random.key(seed), 9)
    return {
        "detail_rows": draw_detail_rows(jax.random.fold_in(streams_of[8], 71), 0),
        "row_block": draw_row_block(jax.random.fold_in(streams_of[8], 71), 0),
        "block_weight": with_ends(jax.random.randint(streams_of[2], (BLOCKS,), 1, 10), jax.random.fold_in(streams_of[2], 1), 1, 9).astype(jnp.int32),
        "block_group": draw_block_group(jax.random.fold_in(streams_of[8], 71), 0),
        "query_matrix": with_ends((jax.random.randint(streams_of[4], (CELLS, QUERIES), 0, 16) < 1).astype(jnp.int32), jax.random.fold_in(streams_of[4], 1), 0, 1),
        "query_weight": jnp.clip(jnp.exp(jax.random.uniform(streams_of[5], (QUERIES,), jnp.float32, math.log(0.0048828125), math.log(0.048828125))), 0.0048828125, 0.048828125),
        "query_noisy": centred(streams_of[6], (BLOCKS, QUERIES), 8.0, 48.0, ((0, 64),), jnp.float32),
        "group_noisy": centred(streams_of[7], (GROUPS, CELLS), 8.0, 48.0, ((1, 8),), jnp.float32),
    }


AGG_WEIGHT = 0.25
HIGHEST_PREC = lax.Precision.HIGHEST


def reference(detail_rows, row_block, block_weight, block_group, query_matrix, query_weight, query_noisy, group_noisy):
    detail = jnp.zeros(detail_rows.shape, detail_rows.dtype).at[row_block].set(detail_rows)
    weight = block_weight.astype(detail_rows.dtype)[:, None]
    queries = query_matrix.astype(detail_rows.dtype)

    def operate(estimate):
        marginal = jnp.dot(estimate, queries, precision=HIGHEST_PREC, preferred_element_type=jnp.float32) * query_weight[None, :]
        spread_back = jnp.dot(marginal, queries.T, precision=HIGHEST_PREC, preferred_element_type=jnp.float32)
        totals = jax.ops.segment_sum(estimate, block_group, num_segments=GROUPS)
        return weight * estimate + spread_back + AGG_WEIGHT * totals[block_group]

    right_side = weight * detail
    right_side = right_side + jnp.dot(query_noisy * query_weight[None, :], queries.T, precision=HIGHEST_PREC, preferred_element_type=jnp.float32)
    right_side = right_side + AGG_WEIGHT * group_noisy[block_group]
    solution_field = jnp.zeros_like(right_side)
    residual = right_side
    direction = right_side
    norm_now = jnp.sum(residual * residual)
    for iteration in range(ITERS):
        image_vec = operate(direction)
        step_size = norm_now / jnp.sum(direction * image_vec)
        solution_field = solution_field + step_size * direction
        residual = residual - step_size * image_vec
        norm_next = jnp.sum(residual * residual)
        direction = residual + (norm_next / norm_now) * direction
        norm_now = norm_next
    return solution_field, residual
```

```python
import functools
import jax
import jax.numpy as jnp
from jax import lax
from jax.experimental import pallas as pl
from jax.experimental.pallas import tpu as pltpu
from jax.sharding import PartitionSpec as P

NZ, NY, NX, NC = 16, 4, 4, 2
GROUP_SIZE = 128.0
F32, BF16 = jnp.float32, jnp.bfloat16
NN = (((1,), (0,)), ((), ()))
NT = (((1,), (1,)), ((), ()))
TN = (((0,), (0,)), ((), ()))


def parts(x, n):
    out = []
    for i in range(n):
        p = x.astype(BF16)
        out.append(p)
        if i < n - 1:
            x = x - p.astype(F32)
    return out


def mxu(a, b, dims):
    return lax.dot_general(a, b, dims, preferred_element_type=F32)


def dot_l(x, y, dims, n=3):
    return functools.reduce(lambda s, p: s + p, [mxu(p, y, dims) for p in parts(x, n)])


def dot_r(x, y, dims, n=3):
    return functools.reduce(lambda s, p: s + p, [mxu(x, p, dims) for p in parts(y, n)])


def fold(v):
    s = jnp.sum(v, axis=0, keepdims=True)
    return functools.reduce(
        lambda p, q: p + q, [s[:, i : i + 128] for i in range(0, s.shape[1], 128)]
    )


def spread_order(n):
    return sorted(range(1, n), key=lambda k: -min(k, n - k))


def scratch_of(blk, cells, queries, groups):
    share = blk // (NX * NC)
    half = queries // NC
    zr = blk // NZ
    dma = pltpu.SemaphoreType.DMA
    return {
        "qi": pltpu.VMEM((cells, queries), jnp.int32),
        "qb": pltpu.VMEM((cells, queries), BF16),
        "rbv": pltpu.VMEM((1, blk), jnp.int32),
        "bwv": pltpu.VMEM((1, blk), jnp.int32),
        "bgv": pltpu.VMEM((1, blk), jnp.int32),
        "qwv": pltpu.VMEM((1, queries), F32),
        "qnv": pltpu.VMEM((blk, queries), F32),
        "gnv": pltpu.VMEM((groups, cells), F32),
        "ar": pltpu.VMEM((NZ, zr, cells), F32),
        "ai": pltpu.VMEM((NZ, 1, blk), jnp.int32),
        "sy": pltpu.VMEM((NY, zr // NY, NZ, cells), F32),
        "br": pltpu.VMEM((NY, zr // NY, NZ, cells), F32),
        "bi": pltpu.VMEM((NY, NZ, 1, blk), jnp.int32),
        "tp": pltpu.VMEM((groups, 3 * cells + 128), F32),
        "ty": pltpu.VMEM((NY, NZ, 3 * cells + 128), F32),
        "pz": pltpu.VMEM((NZ, 8, 128), F32),
        "tz": pltpu.VMEM((NZ, 8, 128), F32),
        "ex": pltpu.VMEM((16, 128), F32),
        "exr": pltpu.VMEM((NX * NC, 16, 128), F32),
        "mp": pltpu.VMEM((blk, queries), F32),
        "mr": pltpu.VMEM((NX * NC, share, queries), F32),
        "ms": pltpu.VMEM((share, queries), F32),
        "mf": pltpu.VMEM((blk, queries), F32),
        "gp": pltpu.VMEM((queries, queries), F32),
        "gc": pltpu.VMEM((half, queries), F32),
        "gh": pltpu.VMEM((half, queries), F32),
        "gr": pltpu.VMEM((NX, half // NX, queries), F32),
        "gf": pltpu.VMEM((queries, queries), F32),
        "az": pltpu.VMEM((8, 128), F32),
        "azr": pltpu.VMEM((NZ, 8, 128), F32),
        "ay": pltpu.VMEM((NZ, 640), F32),
        "ayr": pltpu.VMEM((NY, NZ, 640), F32),
        "base": pltpu.VMEM((blk, cells), F32),
        "bv": pltpu.VMEM((blk, cells), F32),
        "load": dma((10,)),
        "z_s": dma((NZ,)), "z_r": dma((NZ,)), "zi_s": dma((NZ,)), "zi_r": dma((NZ,)),
        "y_s": dma((NY,)), "y_r": dma((NY,)), "yi_s": dma((NY,)), "yi_r": dma((NY,)),
        "ty_s": dma((NY,)), "ty_r": dma((NY,)),
        "tz_s": dma((NZ,)), "tz_r": dma((NZ,)),
        "ex_s": dma((NX * NC,)), "ex_r": dma((NX * NC,)),
        "mr_s": dma((NX * NC,)), "mr_r": dma((NX * NC,)),
        "ma_s": dma((NX * NC,)), "ma_r": dma((NX * NC,)),
        "gc_s": dma((2,)), "gc_r": dma((2,)),
        "gr_s": dma((NX,)), "gr_r": dma((NX,)),
        "ga_s": dma((NX,)), "ga_r": dma((NX,)),
        "az_s": dma((NZ,)), "az_r": dma((NZ,)),
        "ay_s": dma((NY,)), "ay_r": dma((NY,)),
    }


def kernel(names, dr, rb, bw, bg, qm, qw, qn, gn, x_out, r_out, *refs):
    s = dict(zip(names, refs))
    blk, cells = dr.shape
    queries = qm.shape[1]
    groups = gn.shape[0]
    n_cell = NX * NC
    zr = blk // NZ
    sr = zr // NY
    share = blk // n_cell
    half = queries // NC
    hx = half // NX
    geo = lax.axis_index("geo")
    cell = lax.axis_index("cell")
    z, y = geo // NY, lax.rem(geo, NY)
    x, core = cell // NC, lax.rem(cell, NC)
    mate = 1 - core
    sends = []

    def to_z(k):
        return lax.rem(z + k, NZ)

    def to_y(k):
        return lax.rem(y + k, NY)

    def to_x(k):
        return lax.rem(x + k, NX)

    def to_c(k):
        return lax.rem(cell + k, n_cell)

    def z_peer(k):
        return (to_z(k) * NY + y, cell)

    def y_peer(k):
        return (z * NY + to_y(k), cell)

    def x_peer(k):
        return (geo, to_x(k) * NC + core)

    def c_peer(k):
        return (geo, to_c(k))

    mate_peer = (geo, x * NC + mate)

    def remote(src, dst, name, k, peer):
        return pltpu.make_async_remote_copy(
            src_ref=src,
            dst_ref=dst,
            send_sem=s[name + "_s"].at[k],
            recv_sem=s[name + "_r"].at[k],
            device_id=peer,
            device_id_type=pl.DeviceIdType.MESH,
        )

    def send(*a):
        copy = remote(*a)
        copy.start()
        sends.append(copy)

    def arrived(dst, name, k, peer):
        remote(dst, dst, name, k, peer).wait_recv()

    loads = [
        pltpu.make_async_copy(src, dst, s["load"].at[i])
        for i, (src, dst) in enumerate(
            [
                (qm, s["qi"]),
                (bw, s["bwv"]),
                (bg, s["bgv"]),
                (qw, s["qwv"]),
                (qn, s["qnv"]),
                (gn, s["gnv"]),
                (dr.at[pl.ds(pl.multiple_of(z * zr, zr), zr)], s["ar"].at[z]),
                (rb, s["ai"].at[z]),
            ]
        )
    ]
    for copy in loads:
        copy.start()

    barrier = pltpu.get_barrier_semaphore()
    greet = (
        [z_peer(k) for k in range(1, NZ)]
        + [y_peer(k) for k in range(1, NY)]
        + [c_peer(k) for k in range(1, n_cell)]
    )
    for peer in greet:
        pl.semaphore_signal(barrier, inc=1, device_id=peer, device_id_type=pl.DeviceIdType.MESH)

    loads[0].wait()
    s["qb"][...] = s["qi"][...].astype(F32).astype(BF16)
    qb = s["qb"]
    s["gp"][...] = mxu(qb[...], qb[...], TN)
    pl.semaphore_wait(barrier, len(greet))

    for k in spread_order(NZ):
        row0 = pl.multiple_of(to_z(k) * zr, zr)
        send(dr.at[pl.ds(row0, zr)], s["ar"].at[z], "z", k, z_peer(k))
        send(rb, s["ai"].at[z], "zi", k, z_peer(k))
    send(s["gp"].at[pl.ds(pl.multiple_of(mate * half, half), half)], s["gc"], "gc", 0, mate_peer)

    for copy in loads[1:]:
        copy.wait()
    eye = lax.broadcasted_iota(jnp.int32, (blk, blk), 0) == lax.broadcasted_iota(jnp.int32, (blk, blk), 1)
    w = jnp.sum(jnp.where(eye, s["bwv"][...].astype(F32), 0.0), axis=1, keepdims=True)
    bg_col = jnp.sum(jnp.where(eye, s["bgv"][...].astype(F32), 0.0), axis=1, keepdims=True)
    pick = (bg_col == lax.broadcasted_iota(jnp.int32, (blk, groups), 1).astype(F32)).astype(F32).astype(BF16)
    gather = (s["bgv"][...] == lax.broadcasted_iota(jnp.int32, (groups, blk), 0)).astype(F32).astype(BF16)
    qw_row = s["qwv"][...]
    s["base"][...] = dot_l(s["qnv"][...] * qw_row, qb[...], NT) + 0.25 * dot_r(pick, s["gnv"][...], NN)

    arrived(s["gc"], "gc", 0, mate_peer)
    s["gh"][...] = s["gp"][pl.ds(pl.multiple_of(core * half, half), half)] + s["gc"][...]
    for k in spread_order(NX):
        send(s["gh"].at[pl.ds(pl.multiple_of(to_x(k) * hx, hx), hx)], s["gr"].at[k], "gr", k, x_peer(k))

    for k in spread_order(NZ)[::-1]:
        src = to_z(NZ - k)
        arrived(s["ar"].at[src], "z", k, z_peer(k))
        arrived(s["ai"].at[src], "zi", k, z_peer(k))
    for yy in range(NY):
        for kk in range(sr):
            s["sy"][yy, kk] = s["ar"][:, yy * sr + kk, :]
    for k in spread_order(NY):
        send(s["sy"].at[to_y(k)], s["br"].at[y], "y", k, y_peer(k))
        send(s["ai"], s["bi"].at[y], "yi", k, y_peer(k))
    s["br"][y] = s["sy"][y]
    s["bi"][y] = s["ai"][...]

    for k in range(1, NX):
        arrived(s["gr"].at[k], "gr", k, x_peer(k))
    mine = pl.ds(pl.multiple_of(core * half + x * hx, hx), hx)
    total = s["gh"][pl.ds(pl.multiple_of(x * hx, hx), hx)]
    for k in range(1, NX):
        total = total + s["gr"][k]
    s["gf"][mine] = total
    for k in spread_order(NX):
        send(s["gf"].at[mine], s["gf"].at[mine], "ga", k, x_peer(k))

    for k in spread_order(NY)[::-1]:
        src = to_y(NY - k)
        arrived(s["br"].at[src], "y", k, y_peer(k))
        arrived(s["bi"].at[src], "yi", k, y_peer(k))

    ids = s["bi"][...].reshape(NY * NZ, blk).astype(F32)
    lane = lax.broadcasted_iota(jnp.int32, (NY * NZ, blk), 1)
    id_col = jnp.concatenate(
        [
            jnp.sum(jnp.where(lane == geo * sr + kk, ids, 0.0), axis=1, keepdims=True)
            for kk in range(sr)
        ],
        axis=0,
    )
    rows = jnp.concatenate([s["br"][:, kk].reshape(NY * NZ, cells) for kk in range(sr)], axis=0)
    here = lax.broadcasted_iota(jnp.int32, (blk, blk), 1) + geo * blk
    place = (id_col == here.astype(F32)).astype(F32).astype(BF16)
    detail = dot_r(place, rows, TN)

    b = w * detail + s["base"][...]
    s["bv"][...] = b
    wb = w * b
    wwb = w * wb
    s["tp"][...] = dot_r(
        gather, jnp.concatenate([b, wb, wwb, jnp.broadcast_to(w, (blk, 128))], axis=1), NN
    )
    for k in spread_order(NY):
        send(s["tp"].at[pl.ds(pl.multiple_of(to_y(k) * NZ, NZ), NZ)], s["ty"].at[k], "ty", k, y_peer(k))
    s["mp"][...] = dot_l(b, qb[...], NN)
    for k in range(1, n_cell):
        send(s["mp"].at[pl.ds(pl.multiple_of(to_c(k) * share, share), share)], s["mr"].at[k], "mr", k, c_peer(k))
    scal_b = [fold(b * b), fold(b * wb), fold(wb * wb), fold(wb * wwb)]

    for k in range(1, NY):
        arrived(s["ty"].at[k], "ty", k, y_peer(k))
    t = s["tp"][pl.ds(pl.multiple_of(y * NZ, NZ), NZ)]
    for k in range(1, NY):
        t = t + s["ty"][k]
    for i, row in enumerate([0, 4, 1, 5, 2, 6, 3]):
        s["pz"][:, row, :] = t[:, i * 128 : (i + 1) * 128]
    s["pz"][:, 7, :] = jnp.zeros((NZ, 128), F32)
    for k in spread_order(NZ):
        send(s["pz"].at[to_z(k)], s["tz"].at[k], "tz", k, z_peer(k))

    for k in range(1, n_cell):
        arrived(s["mr"].at[k], "mr", k, c_peer(k))
    own = pl.ds(pl.multiple_of(cell * share, share), share)
    m_own = s["mp"][own]
    for k in range(1, n_cell):
        m_own = m_own + s["mr"][k]
    s["mf"][own] = m_own
    for k in range(1, n_cell):
        send(s["mf"].at[own], s["mf"].at[own], "ma", k, c_peer(k))

    for k in spread_order(NZ)[::-1]:
        arrived(s["tz"].at[k], "tz", k, z_peer(k))
    t = s["pz"][z]
    for k in range(1, NZ):
        t = t + s["tz"][k]
    q0 = dot_l(t, qb[:128], NN)
    q1 = dot_l(t, qb[128:], NN)
    tq = q0[0:2] + q1[4:6]
    t0, t1, t2 = [jnp.concatenate([t[i : i + 1], t[i + 4 : i + 5]], axis=0) for i in range(3)]
    s["ex"][...] = jnp.concatenate(
        [tq[i : i + 1, j : j + 128] for i in range(2) for j in range(0, queries, 128)]
        + scal_b
        + [fold(t0 * t0), fold(t0 * t1), fold(t0 * t2), fold(t1 * t1)],
        axis=0,
    )
    for k in range(1, n_cell):
        send(s["ex"], s["exr"].at[k], "ex", k, c_peer(k))

    for k in range(1, NX):
        src = pl.ds(pl.multiple_of(core * half + to_x(NX - k) * hx, hx), hx)
        arrived(s["gf"].at[src], "ga", k, x_peer(k))
    held = s["gf"].at[pl.ds(pl.multiple_of(core * half, half), half)]
    send(held, held, "gc", 1, mate_peer)

    for k in range(1, n_cell):
        src = pl.ds(pl.multiple_of(to_c(n_cell - k) * share, share), share)
        arrived(s["mf"].at[src], "ma", k, c_peer(k))
    m = s["mf"][...]
    f = m * qw_row
    b = s["bv"][...]
    u = w * b + dot_l(f, qb[...], NT)
    fm = f * m
    sum_fm, sum_wfm, sum_wwfm = fold(fm), fold(w * fm), fold(w * w * fm)

    arrived(s["gf"].at[pl.ds(pl.multiple_of(mate * half, half), half)], "gc", 1, mate_peer)
    g_hi, g_lo = parts(s["gf"][...], 2)
    f3 = parts(f, 3)
    e = mxu(f3[0], g_hi, NN) + mxu(f3[0], g_lo, NN) + mxu(f3[1], g_hi, NN) + mxu(f3[1], g_lo, NN) + mxu(f3[2], g_hi, NN)
    fe = f * e
    sum_fe, sum_wfe, sum_qee = fold(fe), fold(w * fe), fold(qw_row * e * e)
    h = w * m + e
    w2 = w * u + dot_l(h * qw_row, qb[...], NT)

    for k in range(1, n_cell):
        arrived(s["exr"].at[k], "ex", k, c_peer(k))
    ex = s["ex"][...]
    for k in range(1, n_cell):
        ex = ex + s["exr"][k]
    nq = queries // 128
    t0q = jnp.concatenate([ex[i : i + 1] for i in range(nq)], axis=1)
    t1q = jnp.concatenate([ex[nq + i : nq + i + 1] for i in range(nq)], axis=1)
    bb, bwb, wbwb, wbwwb, t00, t01, t02, t11 = [ex[2 * nq + i : 2 * nq + i + 1] for i in range(8)]
    zq = t0q * qw_row
    zq8 = jnp.broadcast_to(zq, (8, queries))
    z3 = parts(zq8, 3)
    zg = (mxu(z3[0], g_hi, NN) + mxu(z3[0], g_lo, NN) + mxu(z3[1], g_hi, NN) + mxu(z3[1], g_lo, NN) + mxu(z3[2], g_hi, NN))[0:1]
    t0k = dot_l(zq8, qb[...], NT)[0:1]
    q00, q01, zgz = fold(zq * t0q), fold(zq * t1q), fold(zg * zq)
    t0k2 = jnp.concatenate([t0k[:, :128], t0k[:, 128:]], axis=0)
    sw = t[3:4]
    gs = GROUP_SIZE
    mu0 = bb
    mu1 = bwb + sum_fm + 0.25 * t00
    mu2 = wbwb + 2.0 * sum_wfm + sum_fe + 0.5 * (t01 + q00) + (gs / 16) * t00
    mu3 = (
        (wbwwb + 2.0 * sum_wwfm + sum_wfe)
        + (sum_wwfm + 2.0 * sum_wfe + sum_qee)
        + 0.5 * (t02 + q01)
        + sw * t00 * (1 / 16)
        + 0.5 * (q01 + zgz)
        + (gs / 16) * q00
        + 0.25 * (t11 + (gs / 2) * t01 + (gs * gs / 16) * t00)
        + 0.5 * (q01 + (gs / 4) * q00)
        + 0.25 * zgz
    )
    s["az"][...] = jnp.concatenate(
        [t0, 0.25 * t1 + 0.5 * t0k2 + (gs / 16) * t0, mu0, mu1, mu2, mu3], axis=0
    )
    s["azr"][z] = s["az"][...]
    for k in spread_order(NZ):
        send(s["az"], s["azr"].at[z], "az", k, z_peer(k))
    for k in spread_order(NZ)[::-1]:
        arrived(s["azr"].at[to_z(NZ - k)], "az", k, z_peer(k))
    for i in range(4):
        s["ay"][:, i * 128 : (i + 1) * 128] = s["azr"][:, i, :]
    mu = jnp.sum(s["azr"][...], axis=0)[4:8]
    s["ay"][:, 512:] = jnp.concatenate([mu] + [jnp.zeros_like(mu)] * (NZ // 4 - 1), axis=0)
    for k in spread_order(NY):
        send(s["ay"], s["ayr"].at[y], "ay", k, y_peer(k))
    s["ayr"][y] = s["ay"][...]
    for k in spread_order(NY)[::-1]:
        arrived(s["ayr"].at[to_y(NY - k)], "ay", k, y_peer(k))

    ayr = s["ayr"][...]
    spread = dot_r(pick, ayr[:, :, :512].reshape(groups, 512), NN)
    mu = jnp.sum(jnp.sum(ayr[:, 0:4, 512:], axis=0), axis=1, keepdims=True)
    mu0, mu1, mu2, mu3 = [mu[i : i + 1] for i in range(4)]
    alpha0 = mu0 / mu1
    rr1 = alpha0 * alpha0 * mu2 - mu0
    up = 1.0 + rr1 / mu0
    alpha1 = rr1 / (up * up * mu1 - 2.0 * alpha0 * up * mu2 + alpha0 * alpha0 * mu3)
    c1 = alpha0 + alpha1 * up
    c2 = alpha0 * alpha1
    t0b = spread[:, :cells]
    w1 = u + 0.25 * t0b
    x_out[...] = c1 * b - c2 * w1
    r_out[...] = b - c1 * w1 + c2 * (w2 + 0.25 * (w * t0b) + spread[:, cells:])

    for copy in sends:
        copy.wait_send()


def local(detail_rows, row_block, block_weight, block_group, query_matrix, query_weight, query_noisy, group_noisy):
    blk, cells = detail_rows.shape
    scratch = scratch_of(blk, cells, query_matrix.shape[1], group_noisy.shape[0])
    out = jax.ShapeDtypeStruct((blk, cells), F32)
    return pl.pallas_call(
        functools.partial(kernel, tuple(scratch)),
        out_shape=(out, out),
        in_specs=[pl.BlockSpec(memory_space=pl.ANY)] * 8,
        out_specs=(pl.BlockSpec(memory_space=pltpu.VMEM),) * 2,
        scratch_shapes=list(scratch.values()),
        compiler_params=pltpu.CompilerParams(
            collective_id=0, has_side_effects=True, vmem_limit_bytes=40 * 1024 * 1024
        ),
    )(
        detail_rows,
        row_block.reshape(1, -1),
        block_weight.reshape(1, -1),
        block_group.reshape(1, -1),
        query_matrix,
        query_weight.reshape(1, -1),
        query_noisy,
        group_noisy,
    )


def solution(mesh):
    return jax.shard_map(
        local,
        mesh=mesh,
        in_specs=(
            P("geo", "cell"),
            P("geo"),
            P("geo"),
            P("geo"),
            P("cell", None),
            P(),
            P("geo", None),
            P(None, "cell"),
        ),
        out_specs=(P("geo", "cell"), P("geo", "cell")),
        check_vma=False,
    )
```

```python
import functools
import jax
import jax.numpy as jnp
from jax import lax
from jax.experimental import pallas as pl
from jax.experimental.pallas import tpu as pltpu
from jax.sharding import PartitionSpec as P

NZ, NY, NX, NC = 16, 4, 4, 2
GROUP_SIZE = 128.0
F32, BF16 = jnp.float32, jnp.bfloat16
NN = (((1,), (0,)), ((), ()))
NT = (((1,), (1,)), ((), ()))
TN = (((0,), (0,)), ((), ()))


def parts(x, n):
    out = []
    for i in range(n):
        p = x.astype(BF16)
        out.append(p)
        if i < n - 1:
            x = x - p.astype(F32)
    return out


def mxu(a, b, dims):
    return lax.dot_general(a, b, dims, preferred_element_type=F32)


def dot_l(x, y, dims, n=3):
    return functools.reduce(lambda s, p: s + p, [mxu(p, y, dims) for p in parts(x, n)])


def dot_r(x, y, dims, n=3):
    return functools.reduce(lambda s, p: s + p, [mxu(x, p, dims) for p in parts(y, n)])


def fold(v):
    s = jnp.sum(v, axis=0, keepdims=True)
    return functools.reduce(
        lambda p, q: p + q, [s[:, i : i + 128] for i in range(0, s.shape[1], 128)]
    )


def spread_order(n):
    return sorted(range(1, n), key=lambda k: -min(k, n - k))


def block_pairs(queries):
    n = queries // 128
    return [(i, j) for i in range(n) for j in range(i, n)]


def scratch_of(blk, cells, queries, groups):
    n_cell = NX * NC
    share = blk // n_cell
    half = len(block_pairs(queries)) * 128 // NC
    hx = half // NX
    zr = blk // NZ
    shapes = {
        "qi": ((cells, queries), jnp.int32),
        "qb": ((cells, queries), BF16),
        "bwv": ((1, blk), jnp.int32),
        "bgv": ((1, blk), jnp.int32),
        "qwv": ((1, queries), F32),
        "qnv": ((blk, queries), F32),
        "gnv": ((groups, cells), F32),
        "ar": ((NZ, zr, cells), F32),
        "ai": ((NZ, 1, blk), jnp.int32),
        "sy": ((NY, zr // NY, NZ, cells), F32),
        "br": ((NY, zr // NY, NZ, cells), F32),
        "bi": ((NY, NZ, 1, blk), jnp.int32),
        "md": ((8, blk), F32),
        "mdr": ((NY, 8, blk), F32),
        "gz": ((groups, NY * blk), BF16),
        "tp": ((groups, 3 * cells), F32),
        "ty": ((NY - 1, NZ, 3 * cells), F32),
        "pz": ((NZ, 8, 128), F32),
        "tz": ((NZ - 1, 8, 128), F32),
        "ex": ((16, 128), F32),
        "exr": ((n_cell - 1, 16, 128), F32),
        "mp": ((blk, queries), F32),
        "mr": ((n_cell - 1, share, queries), F32),
        "ms": ((share, queries), F32),
        "mf": ((blk, queries), F32),
        "gp": ((NC * half, 128), F32),
        "gc": ((half, 128), F32),
        "gh": ((half, 128), F32),
        "gr": ((NX - 1, hx, 128), F32),
        "gs": ((hx, 128), F32),
        "gf": ((NC * half, 128), F32),
        "g_hi": ((queries, queries), BF16),
        "g_lo": ((queries, queries), BF16),
        "az": ((4, 128), F32),
        "azr": ((NZ, 4, 128), F32),
        "ay": ((NZ, 512), F32),
        "ayr": ((NY, NZ, 512), F32),
        "mz": ((4, 128), F32),
        "mzr": ((NZ, 4, 128), F32),
        "my": ((4, 128), F32),
        "myr": ((NY, 4, 128), F32),
        "base": ((blk, cells), F32),
        "bv": ((blk, cells), F32),
        "uv": ((blk, cells), F32),
        "w2l": ((blk, cells), F32),
        "w1v": ((blk, cells), F32),
        "w2v": ((blk, cells), F32),
        "cv": ((8, cells), F32),
    }
    dma = pltpu.SemaphoreType.DMA
    out = {k: pltpu.VMEM(*v) for k, v in shapes.items()}
    out["load"] = dma((6,))
    out["out"] = dma((4,))
    for name in PHASES:
        out[name + "_s"] = dma
        out[name + "_r"] = dma
    return out


PHASES = ("z", "zi", "y", "yi", "md", "ty", "tz", "ex", "mr", "ma", "gc", "gd", "gr", "ga", "az", "ay", "mz", "my")


def kernel(names, dr, rb, bw, bg, qm, qw, qn, gn, b_out, w1_out, w2_out, c_out, *refs):
    s = dict(zip(names, refs))
    blk, cells = dr.shape
    queries = qm.shape[1]
    groups = gn.shape[0]
    n_cell = NX * NC
    zr = blk // NZ
    sr = zr // NY
    share = blk // n_cell
    half = len(block_pairs(queries)) * 128 // NC
    hx = half // NX
    geo = lax.axis_index("geo")
    cell = lax.axis_index("cell")
    z, y = geo // NY, lax.rem(geo, NY)
    x, core = cell // NC, lax.rem(cell, NC)
    mate = 1 - core

    def to_z(k):
        return lax.rem(z + k, NZ)

    def to_y(k):
        return lax.rem(y + k, NY)

    def to_x(k):
        return lax.rem(x + k, NX)

    def to_c(k):
        return lax.rem(cell + k, n_cell)

    def z_peer(k):
        return (to_z(k) * NY + y, cell)

    def y_peer(k):
        return (z * NY + to_y(k), cell)

    def x_peer(k):
        return (geo, to_x(k) * NC + core)

    def c_peer(k):
        return (geo, to_c(k))

    mate_peer = (geo, x * NC + mate)

    def rows(i, n):
        return pl.ds(pl.multiple_of(i * n, n), n)

    def send(src, dst, name, peer):
        pltpu.make_async_remote_copy(
            src_ref=src,
            dst_ref=dst,
            send_sem=s[name + "_s"],
            recv_sem=s[name + "_r"],
            device_id=peer,
            device_id_type=pl.DeviceIdType.MESH,
        ).start()

    def keep(src, dst, name):
        pltpu.make_async_copy(src, dst, s[name + "_r"]).start()

    def arrived(ref, name):
        pltpu.make_async_copy(ref, ref, s[name + "_r"]).wait()

    def sent(ref, name):
        pltpu.make_async_copy(ref, ref, s[name + "_s"]).wait()

    barrier = pltpu.get_barrier_semaphore()
    greet = (
        [z_peer(k) for k in spread_order(NZ)]
        + [y_peer(k) for k in range(1, NY)]
        + [c_peer(k) for k in range(1, n_cell)]
    )
    for peer in greet:
        pl.semaphore_signal(barrier, inc=1, device_id=peer, device_id_type=pl.DeviceIdType.MESH)
    loads = [
        pltpu.make_async_copy(src, s[dst], s["load"].at[i])
        for i, (src, dst) in enumerate([(qm, "qi"), (bw, "bwv"), (bg, "bgv"), (qw, "qwv"), (qn, "qnv"), (gn, "gnv")])
    ]
    for copy in loads:
        copy.start()
    keep(dr.at[rows(z, zr)], s["ar"].at[z], "z")
    keep(rb, s["ai"].at[z], "zi")

    loads[0].wait()
    qb = s["qb"]
    qb[...] = s["qi"][...].astype(F32).astype(BF16)
    pairs = block_pairs(queries)
    at = 0
    for i in range(queries // 128):
        strip = mxu(qb[:, i * 128 : (i + 1) * 128], qb[:, i * 128 :], TN)
        for j in range(0, strip.shape[1], 128):
            s["gp"][at : at + 128] = strip[:, j : j + 128]
            at += 128
    loads[1].wait()
    loads[2].wait()
    w_row = s["bwv"][...].astype(F32)
    bg_row = s["bgv"][...].astype(F32)
    s["md"][...] = jnp.concatenate([w_row, bg_row] + [jnp.zeros_like(w_row)] * 6, axis=0)
    pl.semaphore_wait(barrier, len(greet))

    for k in spread_order(NZ):
        send(dr.at[rows(to_z(k), zr)], s["ar"].at[z], "z", z_peer(k))
        send(rb, s["ai"].at[z], "zi", z_peer(k))
    for k in spread_order(NY):
        send(s["md"], s["mdr"].at[y], "md", y_peer(k))
    keep(s["md"], s["mdr"].at[y], "md")
    send(s["gp"].at[rows(mate, half)], s["gc"], "gc", mate_peer)

    for copy in loads[3:]:
        copy.wait()
    eye = lax.broadcasted_iota(jnp.int32, (blk, blk), 0) == lax.broadcasted_iota(jnp.int32, (blk, blk), 1)
    w = jnp.sum(jnp.where(eye, w_row, 0.0), axis=1, keepdims=True)
    bg_col = jnp.sum(jnp.where(eye, bg_row, 0.0), axis=1, keepdims=True)
    pick = (bg_col == lax.broadcasted_iota(jnp.int32, (blk, groups), 1).astype(F32)).astype(F32).astype(BF16)
    gather = (bg_row == lax.broadcasted_iota(jnp.int32, (groups, blk), 0).astype(F32)).astype(F32).astype(BF16)
    qw_row = s["qwv"][...]
    base = dot_l(s["qnv"][...] * qw_row, qb[...], NT) + 0.25 * dot_r(pick, s["gnv"][...], NN)
    s["base"][...] = base
    s["tp"][...] = dot_r(gather, jnp.concatenate([base, w * base, w * w * base], axis=1), NN)

    arrived(s["gc"], "gc")
    s["gh"][...] = s["gp"][rows(core, half)] + s["gc"][...]
    for k in spread_order(NX):
        send(s["gh"].at[rows(to_x(k), hx)], s["gr"].at[k - 1], "gr", x_peer(k))

    arrived(s["mdr"], "md")
    w_all = jnp.concatenate([s["mdr"][i, 0:1] for i in range(NY)], axis=1)
    bg_all = jnp.concatenate([s["mdr"][i, 1:2] for i in range(NY)], axis=1)
    s["gz"][...] = (
        bg_all == lax.broadcasted_iota(jnp.int32, (groups, NY * blk), 0).astype(F32)
    ).astype(F32).astype(BF16)
    mine = bg_all == (lax.broadcasted_iota(jnp.int32, (NZ, NY * blk), 0) + y * NZ).astype(F32)
    s["pz"][:, 3, :] = jnp.broadcast_to(jnp.sum(jnp.where(mine, w_all, 0.0), axis=1, keepdims=True), (NZ, 128))
    s["pz"][:, 7, :] = jnp.zeros((NZ, 128), F32)

    arrived(s["ar"], "z")
    arrived(s["ai"], "zi")
    for yy in range(NY):
        for kk in range(sr):
            s["sy"][yy, kk] = s["ar"][:, yy * sr + kk, :]
    for k in spread_order(NY):
        send(s["sy"].at[to_y(k)], s["br"].at[y], "y", y_peer(k))
        send(s["ai"], s["bi"].at[y], "yi", y_peer(k))
    keep(s["sy"].at[y], s["br"].at[y], "y")
    keep(s["ai"], s["bi"].at[y], "yi")

    ids = s["ai"][...].reshape(NZ, blk).astype(F32)
    lane = lax.broadcasted_iota(jnp.int32, (NZ, blk), 1)
    id_col = jnp.concatenate(
        [jnp.sum(jnp.where(lane == z * zr + j, ids, 0.0), axis=1, keepdims=True) for j in range(zr)], axis=0
    )
    spot = lax.broadcasted_iota(jnp.int32, (blk, NY * blk), 1) + z * (NY * blk)
    is_at = id_col == spot.astype(F32)
    wr = jnp.sum(jnp.where(is_at, w_all, 0.0), axis=1, keepdims=True)
    of_row = mxu(s["gz"][...], is_at.astype(F32).astype(BF16), NT).astype(BF16)
    r1 = wr * s["sy"][...].reshape(blk, cells)
    r2 = wr * r1
    s["tp"][...] += dot_r(of_row, jnp.concatenate([r1, r2, wr * r2], axis=1), NN)
    for k in spread_order(NY):
        send(s["tp"].at[rows(to_y(k), NZ)], s["ty"].at[k - 1], "ty", y_peer(k))

    arrived(s["gr"], "gr")
    total = s["gh"][rows(x, hx)]
    for k in range(NX - 1):
        total = total + s["gr"][k]
    s["gs"][...] = total
    spot_g = pl.ds(pl.multiple_of(core * half + x * hx, hx), hx)
    for k in spread_order(NX):
        send(s["gs"], s["gf"].at[spot_g], "ga", x_peer(k))
    keep(s["gs"], s["gf"].at[spot_g], "ga")

    arrived(s["br"], "y")
    arrived(s["bi"], "yi")
    ids = s["bi"][...].reshape(NY * NZ, blk).astype(F32)
    lane = lax.broadcasted_iota(jnp.int32, (NY * NZ, blk), 1)
    id_col = jnp.concatenate(
        [
            jnp.sum(jnp.where(lane == geo * sr + kk, ids, 0.0), axis=1, keepdims=True)
            for kk in range(sr)
        ],
        axis=0,
    )
    moved = jnp.concatenate([s["br"][:, kk].reshape(NY * NZ, cells) for kk in range(sr)], axis=0)
    here = lax.broadcasted_iota(jnp.int32, (blk, blk), 1) + geo * blk
    place = (id_col == here.astype(F32)).astype(F32).astype(BF16)
    b = w * dot_r(place, moved, TN) + s["base"][...]
    s["bv"][...] = b
    outs = [pltpu.make_async_copy(s["bv"], b_out, s["out"].at[0])]
    outs[0].start()
    s["mp"][...] = dot_l(b, qb[...], NN)
    for k in range(1, n_cell):
        send(s["mp"].at[rows(to_c(k), share)], s["mr"].at[k - 1], "mr", c_peer(k))

    arrived(s["ty"], "ty")
    t = s["tp"][rows(y, NZ)]
    for k in range(NY - 1):
        t = t + s["ty"][k]
    for i, row in enumerate([0, 4, 1, 5, 2, 6]):
        s["pz"][:, row, :] = t[:, i * 128 : (i + 1) * 128]
    for k in spread_order(NZ):
        send(s["pz"].at[to_z(k)], s["tz"].at[k - 1], "tz", z_peer(k))

    wb = w * b
    scal_b = [fold(b * b), fold(b * wb), fold(wb * wb), fold(wb * (w * wb))]

    arrived(s["mr"], "mr")
    m_own = s["mp"][rows(cell, share)]
    for k in range(n_cell - 1):
        m_own = m_own + s["mr"][k]
    s["ms"][...] = m_own

    held = s["gf"].at[rows(core, half)]
    arrived(held, "ga")
    send(held, held, "gd", mate_peer)

    arrived(s["tz"], "tz")
    t = s["pz"][z]
    for k in range(NZ - 1):
        t = t + s["tz"][k]
    q0 = dot_l(t, qb[:128], NN)
    q1 = dot_l(t, qb[128:], NN)
    tq = q0[0:2] + q1[4:6]
    t0, t1, t2 = [jnp.concatenate([t[i : i + 1], t[i + 4 : i + 5]], axis=0) for i in range(3)]
    s["ex"][...] = jnp.concatenate(
        [tq[i : i + 1, j : j + 128] for i in range(2) for j in range(0, queries, 128)]
        + scal_b
        + [fold(t0 * t0), fold(t0 * t1), fold(t0 * t2), fold(t1 * t1)],
        axis=0,
    )
    for k in range(1, n_cell):
        send(s["ex"], s["exr"].at[k - 1], "ex", c_peer(k))

    for k in range(1, n_cell):
        send(s["ms"], s["mf"].at[rows(cell, share)], "ma", c_peer(k))
    keep(s["ms"], s["mf"].at[rows(cell, share)], "ma")

    arrived(s["gf"].at[rows(mate, half)], "gd")
    for n, (i, j) in enumerate(pairs):
        block = s["gf"][n * 128 : (n + 1) * 128]
        for r, c, v in ((i, j, block), (j, i, block.T))[: 1 + (i < j)]:
            spot = (slice(r * 128, (r + 1) * 128), slice(c * 128, (c + 1) * 128))
            s["g_hi"][spot], s["g_lo"][spot] = parts(v, 2)

    def gram(v):
        p = parts(v, 3)
        hi, lo = s["g_hi"][...], s["g_lo"][...]
        return mxu(p[0], hi, NN) + mxu(p[0], lo, NN) + mxu(p[1], hi, NN) + mxu(p[1], lo, NN) + mxu(p[2], hi, NN)

    arrived(s["exr"], "ex")
    ex = s["ex"][...]
    for k in range(n_cell - 1):
        ex = ex + s["exr"][k]
    nq = queries // 128
    t0q = jnp.concatenate([ex[i : i + 1] for i in range(nq)], axis=1)
    t1q = jnp.concatenate([ex[nq + i : nq + i + 1] for i in range(nq)], axis=1)
    bb, bwb, wbwb, wbwwb, t00, t01, t02, t11 = [ex[2 * nq + i : 2 * nq + i + 1] for i in range(8)]
    zq = t0q * qw_row
    zq8 = jnp.broadcast_to(zq, (8, queries))
    t0k = dot_l(zq8, qb[...], NT)[0:1]
    t0k2 = jnp.concatenate([t0k[:, :128], t0k[:, 128:]], axis=0)
    gs = GROUP_SIZE
    s["az"][...] = jnp.concatenate([t0, 0.25 * t1 + 0.5 * t0k2 + (gs / 16) * t0], axis=0)
    for k in spread_order(NZ):
        send(s["az"], s["azr"].at[z], "az", z_peer(k))
    keep(s["az"], s["azr"].at[z], "az")

    arrived(s["mf"], "ma")
    zg = gram(zq8)[0:1]
    q00, q01, zgz = fold(zq * t0q), fold(zq * t1q), fold(zg * zq)
    sw = t[3:4]
    m = s["mf"][...]
    f = m * qw_row
    fm = f * m
    sum_fm, sum_wfm, sum_wwfm = fold(fm), fold(w * fm), fold(w * w * fm)
    e = gram(f)
    fe = f * e
    sum_fe, sum_wfe, sum_qee = fold(fe), fold(w * fe), fold(qw_row * e * e)
    mu0 = bb
    mu1 = bwb + sum_fm + 0.25 * t00
    mu2 = wbwb + 2.0 * sum_wfm + sum_fe + 0.5 * (t01 + q00) + (gs / 16) * t00
    mu3 = (
        (wbwwb + 2.0 * sum_wwfm + sum_wfe)
        + (sum_wwfm + 2.0 * sum_wfe + sum_qee)
        + 0.5 * (t02 + q01)
        + sw * t00 * (1 / 16)
        + 0.5 * (q01 + zgz)
        + (gs / 16) * q00
        + 0.25 * (t11 + (gs / 2) * t01 + (gs * gs / 16) * t00)
        + 0.5 * (q01 + (gs / 4) * q00)
        + 0.25 * zgz
    )
    s["mz"][...] = jnp.concatenate([mu0, mu1, mu2, mu3], axis=0)
    for k in spread_order(NZ):
        send(s["mz"], s["mzr"].at[z], "mz", z_peer(k))
    keep(s["mz"], s["mzr"].at[z], "mz")
    u = w * s["bv"][...] + dot_l(f, qb[...], NT)
    s["uv"][...] = u
    s["w2l"][...] = w * u + dot_l((w * m + e) * qw_row, qb[...], NT)

    arrived(s["azr"], "az")
    for i in range(4):
        s["ay"][:, i * 128 : (i + 1) * 128] = s["azr"][:, i, :]
    for k in spread_order(NY):
        send(s["ay"], s["ayr"].at[y], "ay", y_peer(k))
    keep(s["ay"], s["ayr"].at[y], "ay")
    arrived(s["mzr"], "mz")
    s["my"][...] = jnp.sum(s["mzr"][...], axis=0)
    for k in spread_order(NY):
        send(s["my"], s["myr"].at[y], "my", y_peer(k))
    keep(s["my"], s["myr"].at[y], "my")
    arrived(s["ayr"], "ay")
    spread = dot_r(pick, s["ayr"][...].reshape(groups, 512), NN)
    t0b = spread[:, :cells]
    s["w1v"][...] = s["uv"][...] + 0.25 * t0b
    s["w2v"][...] = s["w2l"][...] + (0.25 * (w * t0b) + spread[:, cells:])
    outs += [
        pltpu.make_async_copy(s["w1v"], w1_out, s["out"].at[1]),
        pltpu.make_async_copy(s["w2v"], w2_out, s["out"].at[2]),
    ]
    outs[1].start()
    outs[2].start()
    arrived(s["myr"], "my")
    mu = jnp.sum(jnp.sum(s["myr"][...], axis=0), axis=1, keepdims=True)
    mu0, mu1, mu2, mu3 = [mu[i : i + 1] for i in range(4)]
    alpha0 = mu0 / mu1
    rr1 = alpha0 * alpha0 * mu2 - mu0
    up = 1.0 + rr1 / mu0
    alpha1 = rr1 / (up * up * mu1 - 2.0 * alpha0 * up * mu2 + alpha0 * alpha0 * mu3)
    c1 = alpha0 + alpha1 * up
    c2 = alpha0 * alpha1
    s["cv"][...] = jnp.concatenate([jnp.broadcast_to(c, (4, cells)) for c in (c1, c2)], axis=0)
    outs.append(pltpu.make_async_copy(s["cv"], c_out, s["out"].at[3]))
    outs[3].start()

    for name, ref in (
        ("z", s["ar"].at[: NZ - 1]),
        ("zi", s["ai"].at[: NZ - 1]),
        ("y", s["br"].at[: NY - 1]),
        ("yi", s["bi"].at[: NY - 1]),
        ("md", s["mdr"].at[: NY - 1]),
        ("ty", s["ty"]),
        ("tz", s["tz"]),
        ("ex", s["exr"]),
        ("mr", s["mr"]),
        ("ma", s["mr"]),
        ("gc", s["gc"]),
        ("gd", s["gc"]),
        ("gr", s["gr"]),
        ("ga", s["gr"]),
        ("az", s["azr"].at[: NZ - 1]),
        ("ay", s["ayr"].at[: NY - 1]),
        ("mz", s["mzr"].at[: NZ - 1]),
        ("my", s["myr"].at[: NY - 1]),
    ):
        sent(ref, name)
    for copy in outs:
        copy.wait()


def combine(b_in, w1_in, w2_in, c_in, x_out, r_out, b, w1, w2, c, x, r, load, load_c, store):
    blk = b.shape[0]
    steps = store.shape[0]
    n = blk // steps
    get_c = pltpu.make_async_copy(c_in, c, load_c)
    get_c.start()
    gets, puts = [], []
    for i in range(steps):
        part = pl.ds(i * n, n)
        gets.append(
            [
                pltpu.make_async_copy(src.at[part], dst.at[part], load.at[i, j])
                for j, (src, dst) in enumerate(((b_in, b), (w1_in, w1), (w2_in, w2)))
            ]
        )
        for copy in gets[-1]:
            copy.start()
    get_c.wait()
    c1, c2 = c[0:1], c[4:5]
    for i in range(steps):
        part = pl.ds(i * n, n)
        for copy in gets[i]:
            copy.wait()
        x[part] = c1 * b[part] - c2 * w1[part]
        r[part] = b[part] - c1 * w1[part] + c2 * w2[part]
        for j, (src, dst) in enumerate(((x, x_out), (r, r_out))):
            puts.append(pltpu.make_async_copy(src.at[part], dst.at[part], store.at[i, j]))
            puts[-1].start()
    for copy in puts:
        copy.wait()


def local(detail_rows, row_block, block_weight, block_group, query_matrix, query_weight, query_noisy, group_noisy):
    blk, cells = detail_rows.shape
    scratch = scratch_of(blk, cells, query_matrix.shape[1], group_noisy.shape[0])
    out = jax.ShapeDtypeStruct((blk, cells), F32)
    taken = pl.pallas_call(
        functools.partial(kernel, tuple(scratch)),
        out_shape=(out, out, out, jax.ShapeDtypeStruct((8, cells), F32)),
        in_specs=[pl.BlockSpec(memory_space=pl.ANY)] * 8,
        out_specs=(pl.BlockSpec(memory_space=pl.ANY),) * 4,
        scratch_shapes=list(scratch.values()),
        compiler_params=pltpu.CompilerParams(
            collective_id=0, has_side_effects=True, vmem_limit_bytes=60 * 1024 * 1024
        ),
    )(
        detail_rows,
        row_block.reshape(1, -1),
        block_weight.reshape(1, -1),
        block_group.reshape(1, -1),
        query_matrix,
        query_weight.reshape(1, -1),
        query_noisy,
        group_noisy,
    )
    return pl.pallas_call(
        combine,
        out_shape=(out, out),
        in_specs=[pl.BlockSpec(memory_space=pl.ANY)] * 4,
        out_specs=(pl.BlockSpec(memory_space=pl.ANY),) * 2,
        scratch_shapes=[pltpu.VMEM((blk, cells), F32)] * 3
        + [pltpu.VMEM((8, cells), F32)]
        + [pltpu.VMEM((blk, cells), F32)] * 2
        + [pltpu.SemaphoreType.DMA((4, 3)), pltpu.SemaphoreType.DMA, pltpu.SemaphoreType.DMA((4, 2))],
        compiler_params=pltpu.CompilerParams(vmem_limit_bytes=60 * 1024 * 1024),
    )(*taken)


def solution(mesh):
    return jax.shard_map(
        local,
        mesh=mesh,
        in_specs=(
            P("geo", "cell"),
            P("geo"),
            P("geo"),
            P("geo"),
            P("cell", None),
            P(),
            P("geo", None),
            P(None, "cell"),
        ),
        out_specs=(P("geo", "cell"), P("geo", "cell")),
        check_vma=False,
    )
```

```python
import functools
import jax
import jax.numpy as jnp
from jax import lax
from jax.experimental import pallas as pl
from jax.experimental.pallas import tpu as pltpu
from jax.sharding import PartitionSpec as P

NZ, NY, NX, NC = 16, 4, 4, 2
GROUP_SIZE = 128.0
F32, BF16 = jnp.float32, jnp.bfloat16
NN = (((1,), (0,)), ((), ()))
NT = (((1,), (1,)), ((), ()))
TN = (((0,), (0,)), ((), ()))


def parts(x, n):
    out = []
    for i in range(n):
        p = x.astype(BF16)
        out.append(p)
        if i < n - 1:
            x = x - p.astype(F32)
    return out


def mxu(a, b, dims):
    return lax.dot_general(a, b, dims, preferred_element_type=F32)


def dot_l(x, y, dims, n=3):
    return functools.reduce(lambda s, p: s + p, [mxu(p, y, dims) for p in parts(x, n)])


def dot_r(x, y, dims, n=3):
    return functools.reduce(lambda s, p: s + p, [mxu(x, p, dims) for p in parts(y, n)])


def stack(x):
    terms = [p.astype(F32) for p in parts(x, 3)]
    pad = -3 * x.shape[0] % 16
    return jnp.concatenate(terms + [jnp.zeros((pad, x.shape[1]), F32)] * (pad > 0), axis=0).astype(BF16)


def unstack(y, n):
    return y[:n] + y[n : 2 * n] + y[2 * n : 3 * n]


def fold(v):
    s = jnp.sum(v, axis=0, keepdims=True)
    return functools.reduce(
        lambda p, q: p + q, [s[:, i : i + 128] for i in range(0, s.shape[1], 128)]
    )


def spread_order(n):
    return sorted(range(1, n), key=lambda k: -min(k, n - k))


def block_pairs(queries):
    n = queries // 128
    return [(i, j) for i in range(n) for j in range(i, n)]


def scratch_of(blk, cells, queries, groups):
    n_cell = NX * NC
    share = blk // n_cell
    half = len(block_pairs(queries)) * 128 // NC
    hx = half // NX
    zr = blk // NZ
    shapes = {
        "qi": ((cells, queries), jnp.int32),
        "drv": ((blk, cells), F32),
        "rbv": ((1, blk), jnp.int32),
        "qb": ((cells, queries), BF16),
        "bwv": ((1, blk), jnp.int32),
        "bgv": ((1, blk), jnp.int32),
        "qwv": ((1, queries), F32),
        "qnv": ((blk, queries), F32),
        "gnv": ((groups, cells), F32),
        "ar": ((NZ, zr, cells), F32),
        "ai": ((NZ, 1, blk), jnp.int32),
        "sy": ((NY, zr // NY, NZ, cells), F32),
        "br": ((NY, zr // NY, NZ, cells), F32),
        "bi": ((NY, NZ, 1, blk), jnp.int32),
        "md": ((8, blk), F32),
        "mdr": ((NY, 8, blk), F32),
        "gz": ((4 * groups, NY * blk), BF16),
        "tp": ((groups, 3 * cells), F32),
        "ty": ((NY - 1, NZ, 3 * cells), F32),
        "pz": ((NZ, 8, 128), F32),
        "tz": ((NZ - 1, 8, 128), F32),
        "ex": ((16, 128), F32),
        "exr": ((n_cell - 1, 16, 128), F32),
        "mp": ((blk, queries), F32),
        "mr": ((n_cell - 1, share, queries), F32),
        "ms": ((share, queries), F32),
        "mf": ((blk, queries), F32),
        "gp": ((NC * half, 128), F32),
        "gc": ((half, 128), F32),
        "gh": ((half, 128), F32),
        "gr": ((NX - 1, hx, 128), F32),
        "gs": ((hx, 128), F32),
        "gf": ((NC * half, 128), F32),
        "g_hi": ((queries, queries), BF16),
        "g_lo": ((queries, queries), BF16),
        "az": ((4, 128), F32),
        "azr": ((NZ, 4, 128), F32),
        "ayr": ((NY, NZ, 4, 128), F32),
        "mz": ((4, 128), F32),
        "mzr": ((NZ, 4, 128), F32),
        "my": ((4, 128), F32),
        "myr": ((NY, 4, 128), F32),
        "base": ((blk, cells), F32),
        "bv": ((blk, cells), F32),
        "uv": ((blk, cells), F32),
        "w2l": ((blk, cells), F32),
        "w1v": ((blk, cells), F32),
        "w2v": ((blk, cells), F32),
        "xv": ((blk, cells), F32),
        "rv": ((blk, cells), F32),
    }
    dma = pltpu.SemaphoreType.DMA
    out = {k: pltpu.VMEM(*v) for k, v in shapes.items()}
    out["load"] = dma((8,))
    out["out"] = dma((4, 2))
    for name in PHASES:
        out[name + "_s"] = dma
        out[name + "_r"] = dma
    return out


PHASES = ("z", "zi", "y", "yi", "md", "ty", "tz", "ex", "mr", "ma", "gc", "gd", "gr", "ga", "az", "af", "ay", "mz", "my")


FAR = [k for k in range(1, NZ) if min(k, NZ - k) > 5]


def kernel(names, dr, rb, bw, bg, qm, qw, qn, gn, x_out, r_out, *refs):
    s = dict(zip(names, refs))
    blk, cells = dr.shape
    queries = qm.shape[1]
    groups = gn.shape[0]
    n_cell = NX * NC
    zr = blk // NZ
    sr = zr // NY
    share = blk // n_cell
    half = len(block_pairs(queries)) * 128 // NC
    hx = half // NX
    geo = lax.axis_index("geo")
    cell = lax.axis_index("cell")
    z, y = geo // NY, lax.rem(geo, NY)
    x, core = cell // NC, lax.rem(cell, NC)
    mate = 1 - core

    def to_z(k):
        return lax.rem(z + k, NZ)

    def to_y(k):
        return lax.rem(y + k, NY)

    def to_x(k):
        return lax.rem(x + k, NX)

    def to_c(k):
        return lax.rem(cell + k, n_cell)

    def z_peer(k):
        return (to_z(k) * NY + y, cell)

    def y_peer(k):
        return (z * NY + to_y(k), cell)

    def x_peer(k):
        return (geo, to_x(k) * NC + core)

    def c_peer(k):
        return (geo, to_c(k))

    mate_peer = (geo, x * NC + mate)

    def rows(i, n):
        return pl.ds(pl.multiple_of(i * n, n), n)

    def send(src, dst, name, peer):
        pltpu.make_async_remote_copy(
            src_ref=src,
            dst_ref=dst,
            send_sem=s[name + "_s"],
            recv_sem=s[name + "_r"],
            device_id=peer,
            device_id_type=pl.DeviceIdType.MESH,
        ).start()

    def keep(src, dst, name):
        pltpu.make_async_copy(src, dst, s[name + "_r"]).start()

    def arrived(ref, name):
        pltpu.make_async_copy(ref, ref, s[name + "_r"]).wait()

    def sent(ref, name):
        pltpu.make_async_copy(ref, ref, s[name + "_s"]).wait()

    barrier = pltpu.get_barrier_semaphore()
    greet = (
        [z_peer(k) for k in spread_order(NZ)]
        + [y_peer(k) for k in range(1, NY)]
        + [c_peer(k) for k in range(1, n_cell)]
    )
    for peer in greet:
        pl.semaphore_signal(barrier, inc=1, device_id=peer, device_id_type=pl.DeviceIdType.MESH)
    loads = [
        pltpu.make_async_copy(src, s[dst], s["load"].at[i])
        for i, (src, dst) in enumerate([(dr, "drv"), (rb, "rbv"), (qm, "qi"), (bw, "bwv"), (bg, "bgv"), (qw, "qwv"), (qn, "qnv"), (gn, "gnv")])
    ]
    for copy in loads:
        copy.start()
    keep(dr.at[rows(z, zr)], s["ar"].at[z], "z")
    keep(rb, s["ai"].at[z], "zi")

    loads[2].wait()
    qb = s["qb"]
    qb[...] = s["qi"][...].astype(F32).astype(BF16)
    pairs = block_pairs(queries)
    at = 0
    for i in range(queries // 128):
        strip = mxu(qb[:, i * 128 : (i + 1) * 128], qb[:, i * 128 :], TN)
        for j in range(0, strip.shape[1], 128):
            s["gp"][at : at + 128] = strip[:, j : j + 128]
            at += 128
    loads[3].wait()
    loads[4].wait()
    w_row = s["bwv"][...].astype(F32)
    bg_row = s["bgv"][...].astype(F32)
    s["md"][...] = jnp.concatenate([w_row, bg_row] + [jnp.zeros_like(w_row)] * 6, axis=0)
    loads[0].wait()
    loads[1].wait()
    pl.semaphore_wait(barrier, len(greet))

    for k in spread_order(NZ):
        send(s["drv"].at[rows(to_z(k), zr)], s["ar"].at[z], "z", z_peer(k))
        send(s["rbv"], s["ai"].at[z], "zi", z_peer(k))
    for k in spread_order(NY):
        send(s["md"], s["mdr"].at[y], "md", y_peer(k))
    keep(s["md"], s["mdr"].at[y], "md")
    send(s["gp"].at[rows(mate, half)], s["gc"], "gc", mate_peer)

    for copy in loads[5:]:
        copy.wait()
    eye = lax.broadcasted_iota(jnp.int32, (blk, blk), 0) == lax.broadcasted_iota(jnp.int32, (blk, blk), 1)
    w = jnp.sum(jnp.where(eye, w_row, 0.0), axis=1, keepdims=True)
    bg_col = jnp.sum(jnp.where(eye, bg_row, 0.0), axis=1, keepdims=True)
    pick = (bg_col == lax.broadcasted_iota(jnp.int32, (blk, groups), 1).astype(F32)).astype(F32).astype(BF16)
    gather = (bg_row == lax.broadcasted_iota(jnp.int32, (groups, blk), 0).astype(F32)).astype(F32).astype(BF16)
    qw_row = s["qwv"][...]
    base = dot_l(s["qnv"][...] * qw_row, qb[...], NT) + 0.25 * dot_r(pick, s["gnv"][...], NN)
    s["base"][...] = base
    s["tp"][...] = dot_r(gather, jnp.concatenate([base, w * base, w * w * base], axis=1), NN)

    arrived(s["gc"], "gc")
    s["gh"][...] = s["gp"][rows(core, half)] + s["gc"][...]
    for k in spread_order(NX):
        send(s["gh"].at[rows(to_x(k), hx)], s["gr"].at[k - 1], "gr", x_peer(k))

    arrived(s["mdr"], "md")
    w_all = jnp.concatenate([s["mdr"][i, 0:1] for i in range(NY)], axis=1)
    bg_all = jnp.concatenate([s["mdr"][i, 1:2] for i in range(NY)], axis=1)
    is_in = bg_all == lax.broadcasted_iota(jnp.int32, (groups, NY * blk), 0).astype(F32)
    cube = parts(w_all * w_all * w_all, 2)
    for i, v in enumerate([w_all, w_all * w_all, cube[0].astype(F32), cube[1].astype(F32)]):
        s["gz"][i * groups : (i + 1) * groups] = jnp.where(is_in, v, 0.0).astype(BF16)
    mine = bg_all == (lax.broadcasted_iota(jnp.int32, (NZ, NY * blk), 0) + y * NZ).astype(F32)
    s["pz"][:, 3, :] = jnp.broadcast_to(jnp.sum(jnp.where(mine, w_all, 0.0), axis=1, keepdims=True), (NZ, 128))
    s["pz"][:, 7, :] = jnp.zeros((NZ, 128), F32)

    arrived(s["ar"], "z")
    arrived(s["ai"], "zi")
    for yy in range(NY):
        for kk in range(sr):
            s["sy"][yy, kk] = s["ar"][:, yy * sr + kk, :]
    for k in spread_order(NY):
        send(s["sy"].at[to_y(k)], s["br"].at[y], "y", y_peer(k))
        send(s["ai"], s["bi"].at[y], "yi", y_peer(k))
    keep(s["sy"].at[y], s["br"].at[y], "y")
    keep(s["ai"], s["bi"].at[y], "yi")

    ids = s["ai"][...].reshape(NZ, blk).astype(F32)
    lane = lax.broadcasted_iota(jnp.int32, (NZ, blk), 1)
    id_col = jnp.concatenate(
        [jnp.sum(jnp.where(lane == z * zr + j, ids, 0.0), axis=1, keepdims=True) for j in range(zr)], axis=0
    )
    spot = lax.broadcasted_iota(jnp.int32, (blk, NY * blk), 1) + z * (NY * blk)
    is_at = id_col == spot.astype(F32)
    of_row = mxu(s["gz"][...], is_at.astype(F32).astype(BF16), NT).astype(BF16)
    sums = dot_r(of_row, s["sy"][...].reshape(blk, cells), NN)
    s["tp"][:, :cells] += sums[:groups]
    s["tp"][:, cells : 2 * cells] += sums[groups : 2 * groups]
    s["tp"][:, 2 * cells :] += sums[2 * groups : 3 * groups] + sums[3 * groups :]
    for k in spread_order(NY):
        send(s["tp"].at[rows(to_y(k), NZ)], s["ty"].at[k - 1], "ty", y_peer(k))

    arrived(s["gr"], "gr")
    total = s["gh"][rows(x, hx)]
    for k in range(NX - 1):
        total = total + s["gr"][k]
    s["gs"][...] = total
    spot_g = pl.ds(pl.multiple_of(core * half + x * hx, hx), hx)
    for k in spread_order(NX):
        send(s["gs"], s["gf"].at[spot_g], "ga", x_peer(k))
    keep(s["gs"], s["gf"].at[spot_g], "ga")

    arrived(s["br"], "y")
    arrived(s["bi"], "yi")
    ids = s["bi"][...].reshape(NY * NZ, blk).astype(F32)
    lane = lax.broadcasted_iota(jnp.int32, (NY * NZ, blk), 1)
    id_col = jnp.concatenate(
        [
            jnp.sum(jnp.where(lane == geo * sr + kk, ids, 0.0), axis=1, keepdims=True)
            for kk in range(sr)
        ],
        axis=0,
    )
    moved = jnp.concatenate([s["br"][:, kk].reshape(NY * NZ, cells) for kk in range(sr)], axis=0)
    here = lax.broadcasted_iota(jnp.int32, (blk, blk), 1) + geo * blk
    place = (id_col == here.astype(F32)).astype(F32).astype(BF16)
    b = w * dot_r(place, moved, TN) + s["base"][...]
    s["bv"][...] = b
    s["mp"][...] = dot_l(b, qb[...], NN)
    for k in range(1, n_cell):
        send(s["mp"].at[rows(to_c(k), share)], s["mr"].at[k - 1], "mr", c_peer(k))

    arrived(s["ty"], "ty")
    t = s["tp"][rows(y, NZ)]
    for k in range(NY - 1):
        t = t + s["ty"][k]
    for i, row in enumerate([0, 4, 1, 5, 2, 6]):
        s["pz"][:, row, :] = t[:, i * 128 : (i + 1) * 128]
    for k in spread_order(NZ):
        send(s["pz"].at[to_z(k)], s["tz"].at[k - 1], "tz", z_peer(k))

    wb = w * b
    scal_b = [fold(b * b), fold(b * wb), fold(wb * wb), fold(wb * (w * wb))]

    arrived(s["mr"], "mr")
    m_own = s["mp"][rows(cell, share)]
    for k in range(n_cell - 1):
        m_own = m_own + s["mr"][k]
    s["ms"][...] = m_own
    for k in range(1, n_cell):
        send(s["ms"], s["mf"].at[rows(cell, share)], "ma", c_peer(k))
    keep(s["ms"], s["mf"].at[rows(cell, share)], "ma")

    held = s["gf"].at[rows(core, half)]
    arrived(held, "ga")
    send(held, held, "gd", mate_peer)

    arrived(s["tz"], "tz")
    t = s["pz"][z]
    for k in range(NZ - 1):
        t = t + s["tz"][k]
    tq = unstack(mxu(stack(jnp.concatenate([t[0:2], t[4:6]], axis=1)), qb[...], NN), 2)
    t0, t1, t2 = [jnp.concatenate([t[i : i + 1], t[i + 4 : i + 5]], axis=0) for i in range(3)]
    s["ex"][...] = jnp.concatenate(
        [tq[i : i + 1, j : j + 128] for i in range(2) for j in range(0, queries, 128)]
        + scal_b
        + [fold(t0 * t0), fold(t0 * t1), fold(t0 * t2), fold(t1 * t1)],
        axis=0,
    )
    for k in range(1, n_cell):
        send(s["ex"], s["exr"].at[k - 1], "ex", c_peer(k))

    arrived(s["gf"].at[rows(mate, half)], "gd")
    for n, (i, j) in enumerate(pairs):
        block = s["gf"][n * 128 : (n + 1) * 128]
        for r, c, v in ((i, j, block), (j, i, block.T))[: 1 + (i < j)]:
            spot = (slice(r * 128, (r + 1) * 128), slice(c * 128, (c + 1) * 128))
            s["g_hi"][spot], s["g_lo"][spot] = parts(v, 2)

    def gram(v):
        p = parts(v, 3)
        hi, lo = s["g_hi"][...], s["g_lo"][...]
        return mxu(p[0], hi, NN) + mxu(p[0], lo, NN) + mxu(p[1], hi, NN) + mxu(p[1], lo, NN) + mxu(p[2], hi, NN)

    arrived(s["mf"], "ma")
    m = s["mf"][...]
    f = m * qw_row
    fm = f * m
    sum_fm, sum_wfm, sum_wwfm = fold(fm), fold(w * fm), fold(w * w * fm)
    e = gram(f)
    fe = f * e
    sum_fe, sum_wfe, sum_qee = fold(fe), fold(w * fe), fold(qw_row * e * e)
    arrived(s["exr"], "ex")
    ex = s["ex"][...]
    for k in range(n_cell - 1):
        ex = ex + s["exr"][k]
    nq = queries // 128
    t0q = jnp.concatenate([ex[i : i + 1] for i in range(nq)], axis=1)
    t1q = jnp.concatenate([ex[nq + i : nq + i + 1] for i in range(nq)], axis=1)
    bb, bwb, wbwb, wbwwb, t00, t01, t02, t11 = [ex[2 * nq + i : 2 * nq + i + 1] for i in range(8)]
    zq = t0q * qw_row
    z3 = stack(zq)
    t0k = unstack(mxu(z3, qb[...], NT), 1)
    t0k2 = jnp.concatenate([t0k[:, :128], t0k[:, 128:]], axis=0)
    gs = GROUP_SIZE
    s["az"][...] = jnp.concatenate([t0, 0.25 * t1 + 0.5 * t0k2 + (gs / 16) * t0], axis=0)
    for k in spread_order(NZ):
        send(s["az"], s["azr"].at[z], "af" if k in FAR else "az", z_peer(k))
    keep(s["az"], s["azr"].at[z], "az")

    zg = unstack(mxu(z3, s["g_hi"][...], NN) + mxu(z3, s["g_lo"][...], NN), 1)
    q00, q01, zgz = fold(zq * t0q), fold(zq * t1q), fold(zg * zq)
    sw = t[3:4]
    mu0 = bb
    mu1 = bwb + sum_fm + 0.25 * t00
    mu2 = wbwb + 2.0 * sum_wfm + sum_fe + 0.5 * (t01 + q00) + (gs / 16) * t00
    mu3 = (
        (wbwwb + 2.0 * sum_wwfm + sum_wfe)
        + (sum_wwfm + 2.0 * sum_wfe + sum_qee)
        + 0.5 * (t02 + q01)
        + sw * t00 * (1 / 16)
        + 0.5 * (q01 + zgz)
        + (gs / 16) * q00
        + 0.25 * (t11 + (gs / 2) * t01 + (gs * gs / 16) * t00)
        + 0.5 * (q01 + (gs / 4) * q00)
        + 0.25 * zgz
    )
    s["mz"][...] = jnp.concatenate([mu0, mu1, mu2, mu3], axis=0)
    for k in spread_order(NZ):
        send(s["mz"], s["mzr"].at[z], "mz", z_peer(k))
    keep(s["mz"], s["mzr"].at[z], "mz")
    u = w * s["bv"][...] + dot_l(f, qb[...], NT)
    s["uv"][...] = u
    s["w2l"][...] = w * u + dot_l((w * m + e) * qw_row, qb[...], NT)

    n_far = len(FAR)
    arrived(s["azr"].at[: NZ - n_far], "az")
    for k in range(NZ):
        if k not in FAR:
            for j in spread_order(NY):
                send(s["azr"].at[to_z(k)], s["ayr"].at[y, to_z(k)], "ay", y_peer(j))
    arrived(s["azr"].at[:n_far], "af")
    for k in FAR:
        for j in spread_order(NY):
            send(s["azr"].at[to_z(k)], s["ayr"].at[y, to_z(k)], "ay", y_peer(j))
    keep(s["azr"], s["ayr"].at[y], "ay")
    arrived(s["mzr"], "mz")
    s["my"][...] = jnp.sum(s["mzr"][...], axis=0)
    for k in spread_order(NY):
        send(s["my"], s["myr"].at[y], "my", y_peer(k))
    keep(s["my"], s["myr"].at[y], "my")
    arrived(s["ayr"], "ay")
    gathered = jnp.concatenate([s["ayr"][:, :, i, :].reshape(groups, 128) for i in range(4)], axis=1)
    spread = dot_r(pick, gathered, NN)
    t0b = spread[:, :cells]
    s["w1v"][...] = s["uv"][...] + 0.25 * t0b
    s["w2v"][...] = s["w2l"][...] + (0.25 * (w * t0b) + spread[:, cells:])
    arrived(s["myr"], "my")
    mu = jnp.sum(jnp.sum(s["myr"][...], axis=0), axis=1, keepdims=True)
    mu0, mu1, mu2, mu3 = [mu[i : i + 1] for i in range(4)]
    alpha0 = mu0 / mu1
    rr1 = alpha0 * alpha0 * mu2 - mu0
    up = 1.0 + rr1 / mu0
    alpha1 = rr1 / (up * up * mu1 - 2.0 * alpha0 * up * mu2 + alpha0 * alpha0 * mu3)
    c1 = alpha0 + alpha1 * up
    c2 = alpha0 * alpha1
    outs = []
    for i in range(4):
        part = slice(i * blk // 4, (i + 1) * blk // 4)
        s["xv"][part] = c1 * s["bv"][part] - c2 * s["w1v"][part]
        s["rv"][part] = s["bv"][part] - c1 * s["w1v"][part] + c2 * s["w2v"][part]
        for j, (src, dst) in enumerate(((s["xv"], x_out), (s["rv"], r_out))):
            outs.append(pltpu.make_async_copy(src.at[part], dst.at[part], s["out"].at[i, j]))
            outs[-1].start()

    for name, ref in (
        ("z", s["ar"].at[: NZ - 1]),
        ("zi", s["ai"].at[: NZ - 1]),
        ("y", s["br"].at[: NY - 1]),
        ("yi", s["bi"].at[: NY - 1]),
        ("md", s["mdr"].at[: NY - 1]),
        ("ty", s["ty"]),
        ("tz", s["tz"]),
        ("ex", s["exr"]),
        ("mr", s["mr"]),
        ("ma", s["mr"]),
        ("gc", s["gc"]),
        ("gd", s["gc"]),
        ("gr", s["gr"]),
        ("ga", s["gr"]),
        ("az", s["azr"].at[: NZ - 1 - n_far]),
        ("af", s["azr"].at[:n_far]),
        ("ay", s["ayr"].at[: NY - 1]),
        ("mz", s["mzr"].at[: NZ - 1]),
        ("my", s["myr"].at[: NY - 1]),
    ):
        sent(ref, name)
    for copy in outs:
        copy.wait()


def hand_on(x_in, r_in, x_out, r_out, x, r, load, store):
    steps = load.shape[0]
    n = x.shape[0] // steps
    moves = []
    for i in range(steps):
        part = pl.ds(i * n, n)
        for j, (src, via, dst) in enumerate(((x_in, x, x_out), (r_in, r, r_out))):
            get = pltpu.make_async_copy(src.at[part], via.at[part], load.at[i, j])
            get.start()
            moves.append((get, pltpu.make_async_copy(via.at[part], dst.at[part], store.at[i, j])))
    for get, put in moves:
        get.wait()
        put.start()
    for get, put in moves:
        put.wait()


def local(detail_rows, row_block, block_weight, block_group, query_matrix, query_weight, query_noisy, group_noisy):
    blk, cells = detail_rows.shape
    scratch = scratch_of(blk, cells, query_matrix.shape[1], group_noisy.shape[0])
    out = jax.ShapeDtypeStruct((blk, cells), F32)
    taken = pl.pallas_call(
        functools.partial(kernel, tuple(scratch)),
        out_shape=(out, out),
        in_specs=[pl.BlockSpec(memory_space=pl.ANY)] * 8,
        out_specs=(pl.BlockSpec(memory_space=pl.ANY),) * 2,
        scratch_shapes=list(scratch.values()),
        compiler_params=pltpu.CompilerParams(
            collective_id=0, has_side_effects=True, vmem_limit_bytes=60 * 1024 * 1024
        ),
    )(
        detail_rows,
        row_block.reshape(1, -1),
        block_weight.reshape(1, -1),
        block_group.reshape(1, -1),
        query_matrix,
        query_weight.reshape(1, -1),
        query_noisy,
        group_noisy,
    )
    return pl.pallas_call(
        hand_on,
        out_shape=(out, out),
        in_specs=[pl.BlockSpec(memory_space=pl.ANY)] * 2,
        out_specs=(pl.BlockSpec(memory_space=pl.ANY),) * 2,
        scratch_shapes=[pltpu.VMEM((blk, cells), F32)] * 2 + [pltpu.SemaphoreType.DMA((2, 2))] * 2,
        compiler_params=pltpu.CompilerParams(vmem_limit_bytes=60 * 1024 * 1024),
    )(*taken)


def solution(mesh):
    return jax.shard_map(
        local,
        mesh=mesh,
        in_specs=(
            P("geo", "cell"),
            P("geo"),
            P("geo"),
            P("geo"),
            P("cell", None),
            P(),
            P("geo", None),
            P(None, "cell"),
        ),
        out_specs=(P("geo", "cell"), P("geo", "cell")),
        check_vma=False,
    )
```

```python
import functools
import jax
import jax.numpy as jnp
from jax import lax
from jax.experimental import pallas as pl
from jax.experimental.pallas import tpu as pltpu
from jax.sharding import PartitionSpec as P

NZ, NY, NX, NC = 16, 4, 4, 2
GROUP_SIZE = 128.0
F32, BF16 = jnp.float32, jnp.bfloat16
NN = (((1,), (0,)), ((), ()))
NT = (((1,), (1,)), ((), ()))
TN = (((0,), (0,)), ((), ()))


def parts(x, n):
    out = []
    for i in range(n):
        p = x.astype(BF16)
        out.append(p)
        if i < n - 1:
            x = x - p.astype(F32)
    return out


def mxu(a, b, dims):
    return lax.dot_general(a, b, dims, preferred_element_type=F32)


def dot_l(x, y, dims, n=3):
    return functools.reduce(lambda s, p: s + p, [mxu(p, y, dims) for p in parts(x, n)])


def dot_r(x, y, dims, n=3):
    return functools.reduce(lambda s, p: s + p, [mxu(x, p, dims) for p in parts(y, n)])


def stack(x):
    terms = [p.astype(F32) for p in parts(x, 3)]
    pad = -3 * x.shape[0] % 16
    return jnp.concatenate(terms + [jnp.zeros((pad, x.shape[1]), F32)] * (pad > 0), axis=0).astype(BF16)


def unstack(y, n):
    return y[:n] + y[n : 2 * n] + y[2 * n : 3 * n]


def fold(v):
    s = jnp.sum(v, axis=0, keepdims=True)
    return functools.reduce(
        lambda p, q: p + q, [s[:, i : i + 128] for i in range(0, s.shape[1], 128)]
    )


def spread_order(n):
    return sorted(range(1, n), key=lambda k: -min(k, n - k))


def block_pairs(queries):
    n = queries // 128
    return [(i, j) for i in range(n) for j in range(i, n)]


def scratch_of(blk, cells, queries, groups):
    n_cell = NX * NC
    share = blk // n_cell
    half = len(block_pairs(queries)) * 128 // NC
    hx = half // NX
    zr = blk // NZ
    shapes = {
        "qi": ((cells, queries), jnp.int32),
        "drv": ((NZ, zr, cells), F32),
        "rbv": ((1, blk), jnp.int32),
        "qb": ((cells, queries), BF16),
        "bwv": ((1, blk), jnp.int32),
        "bgv": ((1, blk), jnp.int32),
        "qwv": ((1, queries), F32),
        "qnv": ((blk, queries), F32),
        "gnv": ((groups, cells), F32),
        "ar": ((NZ, zr, cells), F32),
        "ai": ((NZ, NY, 1, blk), jnp.int32),
        "zs": ((NZ, zr, cells), F32),
        "sy": ((NY, zr // NY, NZ, cells), F32),
        "br": ((NY, zr // NY, NZ, cells), F32),
        "bi": ((NY, 1, blk), jnp.int32),
        "md": ((8, blk), F32),
        "mdr": ((NY, 8, blk), F32),
        "me": ((2, blk), F32),
        "mer": ((NZ, 2, blk), F32),
        "mx": ((8, 128), F32),
        "mxr": ((n_cell - 1, 8, 128), F32),
        "wv": ((blk, 128), F32),
        "tp": ((groups, 3 * cells), F32),
        "ty": ((NY - 1, NZ, 3 * cells), F32),
        "pz": ((NZ, 8, 128), F32),
        "tz": ((NZ - 1, 8, 128), F32),
        "ex": ((16, 128), F32),
        "exr": ((n_cell - 1, 16, 128), F32),
        "mp": ((blk, queries), F32),
        "mr": ((n_cell - 1, share, queries), F32),
        "ms": ((share, queries), F32),
        "mf": ((blk, queries), F32),
        "gp": ((NC * half, 128), F32),
        "gc": ((half, 128), F32),
        "gh": ((half, 128), F32),
        "gr": ((NX - 1, hx, 128), F32),
        "gs": ((hx, 128), F32),
        "gf": ((NC * half, 128), F32),
        "g_hi": ((queries, queries), BF16),
        "g_lo": ((queries, queries), BF16),
        "az": ((4, 128), F32),
        "azr": ((NZ, 4, 128), F32),
        "ayr": ((NY, NZ, 4, 128), F32),
        "mz": ((4, 128), F32),
        "mzr": ((NZ, 4, 128), F32),
        "my": ((4, 128), F32),
        "myr": ((NY, 4, 128), F32),
        "base": ((blk, cells), F32),
        "bv": ((blk, cells), F32),
        "uv": ((blk, cells), F32),
        "w2l": ((blk, cells), F32),
        "w1v": ((blk, cells), F32),
        "w2v": ((blk, cells), F32),
        "xv": ((blk, cells), F32),
        "rv": ((blk, cells), F32),
    }
    dma = pltpu.SemaphoreType.DMA
    out = {k: pltpu.VMEM(*v) for k, v in shapes.items()}
    out["load"] = dma((8,))
    out["out"] = dma((4, 2))
    for name in PHASES:
        out[name + "_s"] = dma
        out[name + "_r"] = dma
    return out


PHASES = ("me", "mx", "z", "zi", "y", "yi", "md", "ty", "tz", "ex", "mr", "ma", "gc", "gd", "gr", "ga", "az", "af", "ay", "mz", "my")


def far_along_z():
    return [k for k in range(1, NZ) if min(k, NZ - k) > 5 * NZ // 16]


def kernel(names, dr, rb, bw, bg, qm, qw, qn, gn, x_out, r_out, *refs):
    s = dict(zip(names, refs))
    blk, cells = rb.shape[1], dr.shape[2]
    queries = qm.shape[1]
    groups = gn.shape[0]
    n_cell = NX * NC
    zr = blk // NZ
    sr = zr // NY
    share = blk // n_cell
    half = len(block_pairs(queries)) * 128 // NC
    hx = half // NX
    geo = lax.axis_index("geo")
    cell = lax.axis_index("cell")
    z, y = geo // NY, lax.rem(geo, NY)
    x, core = cell // NC, lax.rem(cell, NC)
    mate = 1 - core
    far = far_along_z()

    def to_z(k):
        return lax.rem(z + k, NZ)

    def to_y(k):
        return lax.rem(y + k, NY)

    def to_x(k):
        return lax.rem(x + k, NX)

    def to_c(k):
        return lax.rem(cell + k, n_cell)

    def z_peer(k):
        return (to_z(k) * NY + y, cell)

    def y_peer(k):
        return (z * NY + to_y(k), cell)

    def x_peer(k):
        return (geo, to_x(k) * NC + core)

    def c_peer(k):
        return (geo, to_c(k))

    mate_peer = (geo, x * NC + mate)

    def rows(i, n):
        return pl.ds(pl.multiple_of(i * n, n), n)

    def send(src, dst, name, peer):
        pltpu.make_async_remote_copy(
            src_ref=src,
            dst_ref=dst,
            send_sem=s[name + "_s"],
            recv_sem=s[name + "_r"],
            device_id=peer,
            device_id_type=pl.DeviceIdType.MESH,
        ).start()

    def keep(src, dst, name):
        pltpu.make_async_copy(src, dst, s[name + "_r"]).start()

    def arrived(ref, name):
        pltpu.make_async_copy(ref, ref, s[name + "_r"]).wait()

    def sent(ref, name):
        pltpu.make_async_copy(ref, ref, s[name + "_s"]).wait()

    barrier = pltpu.get_barrier_semaphore()
    greet = (
        [z_peer(k) for k in spread_order(NZ)]
        + [y_peer(k) for k in range(1, NY)]
        + [c_peer(k) for k in range(1, n_cell)]
    )
    for peer in greet:
        pl.semaphore_signal(barrier, inc=1, device_id=peer, device_id_type=pl.DeviceIdType.MESH)
    loads = [
        pltpu.make_async_copy(src, s[dst], s["load"].at[i])
        for i, (src, dst) in enumerate([(dr, "drv"), (rb, "rbv"), (qm, "qi"), (bw, "bwv"), (bg, "bgv"), (qw, "qwv"), (qn, "qnv"), (gn, "gnv")])
    ]
    for copy in loads:
        copy.start()
    loads[2].wait()
    qb = s["qb"]
    qb[...] = s["qi"][...].astype(F32).astype(BF16)
    pairs = block_pairs(queries)
    at = 0
    for i in range(queries // 128):
        strip = mxu(qb[:, i * 128 : (i + 1) * 128], qb[:, i * 128 :], TN)
        for j in range(0, strip.shape[1], 128):
            s["gp"][at : at + 128] = strip[:, j : j + 128]
            at += 128
    loads[3].wait()
    loads[4].wait()
    w_row = s["bwv"][...].astype(F32)
    bg_row = s["bgv"][...].astype(F32)
    s["me"][...] = jnp.concatenate([w_row, bg_row], axis=0)
    s["md"][...] = jnp.concatenate([w_row, bg_row] + [jnp.zeros_like(w_row)] * 6, axis=0)
    loads[0].wait()
    loads[1].wait()
    for yy in range(NY):
        for kk in range(sr):
            s["sy"][yy, kk] = s["drv"][:, yy * sr + kk, :]
    pl.semaphore_wait(barrier, len(greet))

    for k in spread_order(NY):
        send(s["sy"].at[to_y(k)], s["br"].at[y], "y", y_peer(k))
        send(s["rbv"], s["bi"].at[y], "yi", y_peer(k))
    for k in spread_order(NZ):
        send(s["me"], s["mer"].at[z], "me", z_peer(k))
    keep(s["sy"].at[y], s["br"].at[y], "y")
    keep(s["rbv"], s["bi"].at[y], "yi")
    keep(s["me"], s["mer"].at[z], "me")
    for k in spread_order(NY):
        send(s["md"], s["mdr"].at[y], "md", y_peer(k))
    keep(s["md"], s["mdr"].at[y], "md")
    send(s["gp"].at[rows(mate, half)], s["gc"], "gc", mate_peer)

    for copy in loads[5:]:
        copy.wait()
    eye = lax.broadcasted_iota(jnp.int32, (blk, blk), 0) == lax.broadcasted_iota(jnp.int32, (blk, blk), 1)
    w = jnp.sum(jnp.where(eye, w_row, 0.0), axis=1, keepdims=True)
    s["wv"][...] = jnp.broadcast_to(w, (blk, 128))
    bg_col = jnp.sum(jnp.where(eye, bg_row, 0.0), axis=1, keepdims=True)
    pick = (bg_col == lax.broadcasted_iota(jnp.int32, (blk, groups), 1).astype(F32)).astype(F32).astype(BF16)
    gather = (bg_row == lax.broadcasted_iota(jnp.int32, (groups, blk), 0).astype(F32)).astype(F32).astype(BF16)
    qw_row = s["qwv"][...]
    base = dot_l(s["qnv"][...] * qw_row, qb[...], NT) + 0.25 * dot_r(pick, s["gnv"][...], NN)
    s["base"][...] = base
    s["tp"][...] = dot_r(gather, jnp.concatenate([base, w * base, w * w * base], axis=1), NN)

    arrived(s["gc"], "gc")
    s["gh"][...] = s["gp"][rows(core, half)] + s["gc"][...]
    for k in spread_order(NX):
        send(s["gh"].at[rows(to_x(k), hx)], s["gr"].at[k - 1], "gr", x_peer(k))

    arrived(s["br"], "y")
    arrived(s["bi"], "yi")
    for yy in range(NY):
        for kk in range(sr):
            s["zs"][:, yy * sr + kk, :] = s["br"][yy, kk]
    for k in spread_order(NZ):
        send(s["zs"].at[to_z(k)], s["ar"].at[z], "z", z_peer(k))
        send(s["bi"], s["ai"].at[z], "zi", z_peer(k))
    keep(s["zs"].at[z], s["ar"].at[z], "z")
    keep(s["bi"], s["ai"].at[z], "zi")

    arrived(s["mdr"], "md")
    w_all = jnp.concatenate([s["mdr"][i, 0:1] for i in range(NY)], axis=1)
    bg_all = jnp.concatenate([s["mdr"][i, 1:2] for i in range(NY)], axis=1)
    mine = bg_all == (lax.broadcasted_iota(jnp.int32, (NZ, NY * blk), 0) + y * NZ).astype(F32)
    s["pz"][:, 3, :] = jnp.broadcast_to(jnp.sum(jnp.where(mine, w_all, 0.0), axis=1, keepdims=True), (NZ, 128))
    s["pz"][:, 7, :] = jnp.zeros((NZ, 128), F32)

    by_z = lax.broadcasted_iota(jnp.int32, (NZ, blk), 0) * zr + y * sr
    lane_z = lax.broadcasted_iota(jnp.int32, (NZ, blk), 1)
    id_col = jnp.concatenate(
        [
            jnp.sum(jnp.where(lane_z == by_z + kk, s["bi"][yy].astype(F32), 0.0), axis=1, keepdims=True)
            for yy in range(NY)
            for kk in range(sr)
        ],
        axis=0,
    )
    block_z = lax.rem(lax.broadcasted_iota(jnp.int32, (blk, blk), 0), NZ)
    spot = lax.broadcasted_iota(jnp.int32, (blk, blk), 1) + (block_z * NY + y) * blk
    is_at = id_col == spot.astype(F32)
    arrived(s["mer"], "me")
    w_r, g_r = [
        jnp.sum(jnp.where(is_at, jnp.concatenate([s["mer"][:, i, :]] * zr, axis=0), 0.0), axis=1, keepdims=True)
        for i in range(2)
    ]
    c_hi, c_lo = [p.astype(F32) for p in parts(w_r * w_r * w_r, 2)]
    column = lax.broadcasted_iota(jnp.int32, (blk, 4 * groups), 1)
    power = jnp.where(
        column < 2 * groups,
        jnp.where(column < groups, w_r, w_r * w_r),
        jnp.where(column < 3 * groups, c_hi, c_lo),
    )
    of_row = jnp.where(g_r == lax.rem(column, groups).astype(F32), power, 0.0).astype(BF16)
    sums = dot_r(of_row, s["br"][...].reshape(blk, cells), TN)
    s["tp"][:, :cells] += sums[:groups]
    s["tp"][:, cells : 2 * cells] += sums[groups : 2 * groups]
    s["tp"][:, 2 * cells :] += sums[2 * groups : 3 * groups] + sums[3 * groups :]
    for k in spread_order(NY):
        send(s["tp"].at[rows(to_y(k), NZ)], s["ty"].at[k - 1], "ty", y_peer(k))

    arrived(s["gr"], "gr")
    total = s["gh"][rows(x, hx)]
    for k in range(NX - 1):
        total = total + s["gr"][k]
    s["gs"][...] = total
    spot_g = pl.ds(pl.multiple_of(core * half + x * hx, hx), hx)
    for k in spread_order(NX):
        send(s["gs"], s["gf"].at[spot_g], "ga", x_peer(k))
    keep(s["gs"], s["gf"].at[spot_g], "ga")

    arrived(s["ty"], "ty")
    t = s["tp"][rows(y, NZ)]
    for k in range(NY - 1):
        t = t + s["ty"][k]
    for i, row in enumerate([0, 4, 1, 5, 2, 6]):
        s["pz"][:, row, :] = t[:, i * 128 : (i + 1) * 128]
    for k in spread_order(NZ):
        send(s["pz"].at[to_z(k)], s["tz"].at[k - 1], "tz", z_peer(k))

    arrived(s["ar"], "z")
    arrived(s["ai"], "zi")
    lane_z = lax.broadcasted_iota(jnp.int32, (NZ, blk), 1)
    id_col = jnp.concatenate(
        [
            jnp.sum(
                jnp.where(lane_z == geo * sr + kk, s["ai"][:, yy].reshape(NZ, blk).astype(F32), 0.0),
                axis=1,
                keepdims=True,
            )
            for yy in range(NY)
            for kk in range(sr)
        ],
        axis=0,
    )
    moved = jnp.concatenate([s["ar"][:, j, :] for j in range(zr)], axis=0)
    here = lax.broadcasted_iota(jnp.int32, (blk, blk), 1) + geo * blk
    place = (id_col == here.astype(F32)).astype(F32).astype(BF16)
    b = w * dot_r(place, moved, TN) + s["base"][...]
    s["bv"][...] = b
    s["mp"][...] = dot_l(b, qb[...], NN)
    for k in range(1, n_cell):
        send(s["mp"].at[rows(to_c(k), share)], s["mr"].at[k - 1], "mr", c_peer(k))

    held = s["gf"].at[rows(core, half)]
    arrived(held, "ga")
    send(held, held, "gd", mate_peer)

    wb = w * b
    scal_b = [fold(b * b), fold(b * wb), fold(wb * wb), fold(wb * (w * wb))]

    arrived(s["tz"], "tz")
    t = s["pz"][z]
    for k in range(NZ - 1):
        t = t + s["tz"][k]
    tq = unstack(mxu(stack(jnp.concatenate([t[0:2], t[4:6]], axis=1)), qb[...], NN), 2)
    t0, t1, t2 = [jnp.concatenate([t[i : i + 1], t[i + 4 : i + 5]], axis=0) for i in range(3)]
    s["ex"][...] = jnp.concatenate(
        [tq[i : i + 1, j : j + 128] for i in range(2) for j in range(0, queries, 128)]
        + scal_b
        + [fold(t0 * t0), fold(t0 * t1), fold(t0 * t2), fold(t1 * t1)],
        axis=0,
    )
    for k in range(1, n_cell):
        send(s["ex"], s["exr"].at[k - 1], "ex", c_peer(k))

    arrived(s["gf"].at[rows(mate, half)], "gd")
    for n, (i, j) in enumerate(pairs):
        block = s["gf"][n * 128 : (n + 1) * 128]
        for r, c, v in ((i, j, block), (j, i, block.T))[: 1 + (i < j)]:
            spot = (slice(r * 128, (r + 1) * 128), slice(c * 128, (c + 1) * 128))
            s["g_hi"][spot], s["g_lo"][spot] = parts(v, 2)

    def gram(v):
        p = parts(v, 3)
        hi, lo = s["g_hi"][...], s["g_lo"][...]
        return mxu(p[0], hi, NN) + mxu(p[0], lo, NN) + mxu(p[1], hi, NN) + mxu(p[1], lo, NN) + mxu(p[2], hi, NN)

    arrived(s["mr"], "mr")
    m_own = s["mp"][rows(cell, share)]
    for k in range(n_cell - 1):
        m_own = m_own + s["mr"][k]
    s["ms"][...] = m_own
    w_own = s["wv"][rows(cell, share)][:, :1]
    f = m_own * qw_row
    fm = f * m_own
    f3 = stack(f)
    e = unstack(mxu(f3, s["g_hi"][...], NN) + mxu(f3, s["g_lo"][...], NN), share)
    fe = f * e
    s["mx"][...] = jnp.concatenate(
        [fold(v) for v in (fm, w_own * fm, w_own * w_own * fm, fe, w_own * fe, qw_row * e * e)]
        + [jnp.zeros((2, 128), F32)],
        axis=0,
    )
    for k in range(1, n_cell):
        send(s["mx"], s["mxr"].at[k - 1], "mx", c_peer(k))

    arrived(s["exr"], "ex")
    ex = s["ex"][...]
    for k in range(n_cell - 1):
        ex = ex + s["exr"][k]
    nq = queries // 128
    t0q = jnp.concatenate([ex[i : i + 1] for i in range(nq)], axis=1)
    t1q = jnp.concatenate([ex[nq + i : nq + i + 1] for i in range(nq)], axis=1)
    bb, bwb, wbwb, wbwwb, t00, t01, t02, t11 = [ex[2 * nq + i : 2 * nq + i + 1] for i in range(8)]
    zq = t0q * qw_row
    z3 = stack(zq)
    t0k = unstack(mxu(z3, qb[...], NT), 1)
    t0k2 = jnp.concatenate([t0k[:, :128], t0k[:, 128:]], axis=0)
    gs = GROUP_SIZE
    s["az"][...] = jnp.concatenate([t0, 0.25 * t1 + 0.5 * t0k2 + (gs / 16) * t0], axis=0)
    for k in spread_order(NZ):
        send(s["az"], s["azr"].at[z], "af" if k in far else "az", z_peer(k))
    keep(s["az"], s["azr"].at[z], "az")
    for k in range(1, n_cell):
        send(s["ms"], s["mf"].at[rows(cell, share)], "ma", c_peer(k))
    keep(s["ms"], s["mf"].at[rows(cell, share)], "ma")

    zg = unstack(mxu(z3, s["g_hi"][...], NN) + mxu(z3, s["g_lo"][...], NN), 1)
    q00, q01, zgz = fold(zq * t0q), fold(zq * t1q), fold(zg * zq)
    sw = t[3:4]
    arrived(s["mxr"], "mx")
    mx = s["mx"][...]
    for k in range(n_cell - 1):
        mx = mx + s["mxr"][k]
    sum_fm, sum_wfm, sum_wwfm, sum_fe, sum_wfe, sum_qee = [mx[i : i + 1] for i in range(6)]
    mu0 = bb
    mu1 = bwb + sum_fm + 0.25 * t00
    mu2 = wbwb + 2.0 * sum_wfm + sum_fe + 0.5 * (t01 + q00) + (gs / 16) * t00
    mu3 = (
        (wbwwb + 2.0 * sum_wwfm + sum_wfe)
        + (sum_wwfm + 2.0 * sum_wfe + sum_qee)
        + 0.5 * (t02 + q01)
        + sw * t00 * (1 / 16)
        + 0.5 * (q01 + zgz)
        + (gs / 16) * q00
        + 0.25 * (t11 + (gs / 2) * t01 + (gs * gs / 16) * t00)
        + 0.5 * (q01 + (gs / 4) * q00)
        + 0.25 * zgz
    )
    s["mz"][...] = jnp.concatenate([mu0, mu1, mu2, mu3], axis=0)
    for k in spread_order(NZ):
        send(s["mz"], s["mzr"].at[z], "mz", z_peer(k))
    keep(s["mz"], s["mzr"].at[z], "mz")
    n_far = len(far)
    arrived(s["azr"].at[: NZ - n_far], "az")
    for k in range(NZ):
        if k not in far:
            for j in spread_order(NY):
                send(s["azr"].at[to_z(k)], s["ayr"].at[y, to_z(k)], "ay", y_peer(j))
    arrived(s["azr"].at[:n_far], "af")
    for k in far:
        for j in spread_order(NY):
            send(s["azr"].at[to_z(k)], s["ayr"].at[y, to_z(k)], "ay", y_peer(j))
    keep(s["azr"], s["ayr"].at[y], "ay")
    arrived(s["mzr"], "mz")
    s["my"][...] = jnp.sum(s["mzr"][...], axis=0)
    for k in spread_order(NY):
        send(s["my"], s["myr"].at[y], "my", y_peer(k))
    keep(s["my"], s["myr"].at[y], "my")
    arrived(s["mf"], "ma")
    m = s["mf"][...]
    f = m * qw_row
    e = gram(f)
    u = w * s["bv"][...] + dot_l(f, qb[...], NT)
    s["uv"][...] = u
    s["w2l"][...] = w * u + dot_l((w * m + e) * qw_row, qb[...], NT)

    arrived(s["ayr"], "ay")
    gathered = jnp.concatenate([s["ayr"][:, :, i, :].reshape(groups, 128) for i in range(4)], axis=1)
    spread = dot_r(pick, gathered, NN)
    t0b = spread[:, :cells]
    s["w1v"][...] = s["uv"][...] + 0.25 * t0b
    s["w2v"][...] = s["w2l"][...] + (0.25 * (w * t0b) + spread[:, cells:])
    arrived(s["myr"], "my")
    mu = jnp.sum(jnp.sum(s["myr"][...], axis=0), axis=1, keepdims=True)
    mu0, mu1, mu2, mu3 = [mu[i : i + 1] for i in range(4)]
    alpha0 = mu0 / mu1
    rr1 = alpha0 * alpha0 * mu2 - mu0
    up = 1.0 + rr1 / mu0
    alpha1 = rr1 / (up * up * mu1 - 2.0 * alpha0 * up * mu2 + alpha0 * alpha0 * mu3)
    c1 = alpha0 + alpha1 * up
    c2 = alpha0 * alpha1
    outs = []
    for i in range(4):
        part = slice(i * blk // 4, (i + 1) * blk // 4)
        s["xv"][part] = c1 * s["bv"][part] - c2 * s["w1v"][part]
        s["rv"][part] = s["bv"][part] - c1 * s["w1v"][part] + c2 * s["w2v"][part]
        for j, (src, dst) in enumerate(((s["xv"], x_out), (s["rv"], r_out))):
            outs.append(pltpu.make_async_copy(src.at[part], dst.at[part], s["out"].at[i, j]))
            outs[-1].start()

    for name, ref in (
        ("me", s["mer"].at[: NZ - 1]),
        ("mx", s["mxr"]),
        ("z", s["ar"].at[: NZ - 1]),
        ("zi", s["ai"].at[: NZ - 1]),
        ("y", s["br"].at[: NY - 1]),
        ("yi", s["bi"].at[: NY - 1]),
        ("md", s["mdr"].at[: NY - 1]),
        ("ty", s["ty"]),
        ("tz", s["tz"]),
        ("ex", s["exr"]),
        ("mr", s["mr"]),
        ("ma", s["mr"]),
        ("gc", s["gc"]),
        ("gd", s["gc"]),
        ("gr", s["gr"]),
        ("ga", s["gr"]),
        ("az", s["azr"].at[: NZ - 1 - n_far]),
        ("af", s["azr"].at[:n_far]),
        ("ay", s["ayr"].at[: NY - 1]),
        ("mz", s["mzr"].at[: NZ - 1]),
        ("my", s["myr"].at[: NY - 1]),
    ):
        sent(ref, name)
    for copy in outs:
        copy.wait()


def hand_on(x_in, r_in, x_out, r_out, x, r, load, store):
    steps = load.shape[0]
    n = x.shape[0] // steps
    moves = []
    for i in range(steps):
        part = pl.ds(i * n, n)
        for j, (src, via, dst) in enumerate(((x_in, x, x_out), (r_in, r, r_out))):
            get = pltpu.make_async_copy(src.at[part], via.at[part], load.at[i, j])
            get.start()
            moves.append((get, pltpu.make_async_copy(via.at[part], dst.at[part], store.at[i, j])))
    for get, put in moves:
        get.wait()
        put.start()
    for get, put in moves:
        put.wait()


def local(detail_rows, row_block, block_weight, block_group, query_matrix, query_weight, query_noisy, group_noisy):
    blk, cells = detail_rows.shape
    scratch = scratch_of(blk, cells, query_matrix.shape[1], group_noisy.shape[0])
    out = jax.ShapeDtypeStruct((blk, cells), F32)
    taken = pl.pallas_call(
        functools.partial(kernel, tuple(scratch)),
        out_shape=(out, out),
        in_specs=[pl.BlockSpec(memory_space=pl.ANY)] * 8,
        out_specs=(pl.BlockSpec(memory_space=pl.ANY),) * 2,
        scratch_shapes=list(scratch.values()),
        compiler_params=pltpu.CompilerParams(
            collective_id=0, has_side_effects=True, vmem_limit_bytes=60 * 1024 * 1024
        ),
    )(
        detail_rows.reshape(NZ, -1, cells),
        row_block.reshape(1, -1),
        block_weight.reshape(1, -1),
        block_group.reshape(1, -1),
        query_matrix,
        query_weight.reshape(1, -1),
        query_noisy,
        group_noisy,
    )
    return pl.pallas_call(
        hand_on,
        out_shape=(out, out),
        in_specs=[pl.BlockSpec(memory_space=pl.ANY)] * 2,
        out_specs=(pl.BlockSpec(memory_space=pl.ANY),) * 2,
        scratch_shapes=[pltpu.VMEM((blk, cells), F32)] * 2 + [pltpu.SemaphoreType.DMA((2, 2))] * 2,
        compiler_params=pltpu.CompilerParams(vmem_limit_bytes=60 * 1024 * 1024),
    )(*taken)


def solution(mesh):
    return jax.shard_map(
        local,
        mesh=mesh,
        in_specs=(
            P("geo", "cell"),
            P("geo"),
            P("geo"),
            P("geo"),
            P("cell", None),
            P(),
            P("geo", None),
            P(None, "cell"),
        ),
        out_specs=(P("geo", "cell"), P("geo", "cell")),
        check_vma=False,
    )
```
